512 devices in a mesh: grp: 16 (over z), dev: 32 (over y, x, core).
Axes of the slice: x: 4, y: 4, z: 16, core: 2. Of those that a mesh axis runs over, the one named last changes fastest.
Arguments:
- student_patches: bfloat16 [131072, 256], P(('grp', 'dev')), may hold values from -8 to 8
- teacher_patches: bfloat16 [131072, 256], P(('grp', 'dev')), may hold values from -8 to 8
- mask_rows: int32 [8192], P(('grp', 'dev')), may hold values from 0 to 255, as said below
- student_proto: bfloat16 [131072, 256], P(('grp', 'dev')), may hold values from -2 to 2
- teacher_proto: bfloat16 [131072, 256], P(('grp', 'dev')), may hold values from -2 to 2
Outputs:
- loss: float32 [], replicated
- proto_grad: float32 [131072, 256], P(('grp', 'dev'))
The draws below stay inside these ranges and needn't reach their ends.
Inputs may be any that keep to these rules, and one draw needn't show every extreme that they name: `mask_rows`: each aligned block of 16 entries (those of one device) holds distinct indices of that device's 256 patch tokens.
All inputs are finite; a program needn't handle non-finite values.
Results may differ from the reference program's by a relative error of at most 0.005.
Values may be sent and summed in bfloat16 or wider, within the bound.
No kernel may reach another device: no remote copies, remote signals or barrier semaphores. Data moves between devices by JAX's collectives and lax.ppermute only.
A program may use at most 128 MiB of HBM per device.

```python
import jax
import jax.numpy as jnp
from jax import lax

D = 256
K = 131072
MASK_DEV = 16
PATCH_DEV = 256
ITERS = 3
ROWS = 8192
PATCHES = 131072


cluster_span = 16


def base_table(key):
    centers = jax.random.normal(jax.random.fold_in(key, 101), (K // cluster_span, D), jnp.float32)
    return jnp.repeat(centers, cluster_span, axis=0)


def patch_owner(key, slope):
    uniform = jax.random.uniform(jax.random.fold_in(key, 102), (PATCHES,), jnp.float32, 0.0, 1.0)
    spread = 1.0 + 0.5 * slope
    position = (jnp.sqrt(1.0 + 2.0 * slope * spread * uniform) - 1.0) / slope
    return jnp.clip((position * K).astype(jnp.int32), 0, K - 1)


def draw_student_proto(key, part):
    base = base_table(key)
    key = jax.random.fold_in(key, 1)
    first, second = jax.random.split(key)
    noise = 0.5 * jax.random.normal(first, (K, D), jnp.float32)
    scales = jnp.exp(jax.random.uniform(second, (K, 1), jnp.float32, -1.2, 1.2))
    return jnp.clip((base + noise) * scales * D ** (-0.5), -2.0, 2.0).astype(jnp.bfloat16)


def draw_teacher_proto(key, part):
    base = base_table(key)
    key = jax.random.fold_in(key, 2)
    first, second = jax.random.split(key)
    noise = 0.5 * jax.random.normal(first, (K, D), jnp.float32)
    scales = jnp.exp(jax.random.uniform(second, (K, 1), jnp.float32, -1.2, 1.2))
    return jnp.clip((base + noise) * scales * D ** (-0.5), -2.0, 2.0).astype(jnp.bfloat16)


def draw_teacher_patches(key, part):
    owned = jnp.take(base_table(key), patch_owner(key, 30.0), axis=0)
    key = jax.random.fold_in(key, 3)
    noise = 0.25 * jax.random.normal(key, (PATCHES, D), jnp.float32)
    return jnp.clip(owned + noise, -8.0, 8.0).astype(jnp.bfloat16)


def draw_student_patches(key, part):
    owned = jnp.take(base_table(key), patch_owner(key, 30.0), axis=0)
    key = jax.random.fold_in(key, 4)
    noise = jax.random.normal(key, (PATCHES, D), jnp.float32)
    return jnp.clip(owned + noise, -8.0, 8.0).astype(jnp.bfloat16)


def draw_mask_rows(key, part):
    key = jax.random.fold_in(key, 5)
    blocks = ROWS // MASK_DEV
    keys = jax.random.split(key, blocks)
    orders = jax.vmap(lambda single: jax.random.permutation(single, PATCH_DEV))(keys).astype(jnp.int32)
    offset = jnp.where(jnp.arange(blocks) == 0, PATCH_DEV - 1 - orders[:, 0], 0).astype(jnp.int32)
    orders = (orders + offset[:, None]) % PATCH_DEV
    return orders[:, :MASK_DEV].reshape(-1).astype(jnp.int32)


def setup_inputs(seed: int = 0) -> dict:
    streams_of = jax.random.split(jax.random.key(seed), 6)
    student_patches = draw_student_patches(jax.random.fold_in(streams_of[5], 71), 0)
    teacher_patches = draw_teacher_patches(jax.random.fold_in(streams_of[5], 71), 0)
    mask_rows = draw_mask_rows(jax.random.fold_in(streams_of[5], 71), 0)
    student_proto = draw_student_proto(jax.random.fold_in(streams_of[5], 71), 0)
    teacher_proto = draw_teacher_proto(jax.random.fold_in(streams_of[5], 71), 0)
    return dict(student_patches=student_patches, teacher_patches=teacher_patches, mask_rows=mask_rows, student_proto=student_proto, teacher_proto=teacher_proto)


norm_eps = 1e-06
teacher_scale = 1.0 / 0.07
student_scale = 1.0 / 0.1

def scores(rows, weights):
    return lax.dot_general(rows, weights, (((1,), (1,)), ((), ())), preferred_element_type=jnp.float32)

def unit_rows(values):
    values = values.astype(jnp.float32)
    return values * lax.rsqrt(lax.optimization_barrier(jnp.sum(values * values, axis=1, keepdims=True)) + norm_eps)

def reference(student_patches, teacher_patches, mask_rows, student_proto, teacher_proto):
    picked = mask_rows + jnp.arange(ROWS, dtype=jnp.int32) // MASK_DEV * PATCH_DEV
    student_rows = unit_rows(jnp.take(student_patches, picked, axis=0)).astype(jnp.bfloat16)
    teacher_rows = unit_rows(jnp.take(teacher_patches, picked, axis=0)).astype(jnp.bfloat16)
    proto_f = student_proto.astype(jnp.float32)
    proto_scale = lax.rsqrt(lax.optimization_barrier(jnp.sum(proto_f * proto_f, axis=1, keepdims=True)) + norm_eps)
    unit_student = proto_f * proto_scale
    student_weights = unit_student.astype(jnp.bfloat16)
    teacher_weights = unit_rows(teacher_proto).astype(jnp.bfloat16)
    targets = jnp.exp(scores(teacher_rows, teacher_weights) * teacher_scale)
    for step in range(ITERS):
        targets = targets / lax.optimization_barrier(jnp.sum(targets, axis=0, keepdims=True))
        targets = targets / lax.optimization_barrier(jnp.sum(targets, axis=1, keepdims=True))
    logits = scores(student_rows, student_weights) * student_scale
    expo = jnp.exp(logits)
    total = lax.optimization_barrier(jnp.sum(expo, axis=1))
    loss = (jnp.sum(jnp.log(total)) - jnp.sum(targets * logits)) / ROWS
    slope = ((expo / total[:, None] - targets) * student_scale).astype(jnp.bfloat16)
    unit_grad = lax.dot_general(slope, student_rows, (((0,), (0,)), ((), ())), preferred_element_type=jnp.float32)
    proto_grad = (unit_grad - unit_student * lax.optimization_barrier(jnp.sum(unit_student * unit_grad, axis=1, keepdims=True))) * proto_scale
    return (loss, proto_grad)
```

```python
import jax
import jax.numpy as jnp
from jax import lax
from jax.experimental import pallas as pl
from jax.experimental.pallas import tpu as pltpu
from jax.sharding import Mesh, PartitionSpec as P

ITERS = 3
LANES = 128

norm_eps = 1e-06
teacher_scale = 1.0 / 0.07
student_scale = 1.0 / 0.1

f32 = jnp.float32
bf16 = jnp.bfloat16
NT = (((1,), (1,)), ((), ()))
NN = (((1,), (0,)), ((), ()))


def dot(a, b, dims):
    return lax.dot_general(a, b, dims, preferred_element_type=f32)


def unit_rows(values):
    values = values.astype(f32)
    return values * lax.rsqrt(jnp.sum(values * values, axis=1, keepdims=True) + norm_eps)


def fold(row):
    n = row.shape[1] // LANES
    return jnp.concatenate([row[:, LANES * i : LANES * (i + 1)] for i in range(n)], axis=0)


def unfold(tile):
    return jnp.concatenate([tile[i : i + 1, :] for i in range(tile.shape[0])], axis=1)


def split_rows(row):
    high = row.astype(bf16).astype(f32)
    which = lax.broadcasted_iota(jnp.int32, (16, row.shape[1]), 0)
    return jnp.where(which == 0, high, jnp.where(which == 1, row - high, 0.0)).astype(bf16)


def matvec(row, matrix, dims):
    return jnp.sum(dot(split_rows(row), matrix, dims), axis=0, keepdims=True)


def spread(out_ref, tile):
    for i in range(out_ref.shape[0]):
        out_ref[i] = tile


def total_of(parts_ref):
    total = parts_ref[0]
    for i in range(1, parts_ref.shape[0]):
        total = total + parts_ref[i]
    return total


def prepare_kernel(mask_ref, sp_ref, tp_ref, sw_ref, tw_ref, rows_ref, weights_ref):
    count = mask_ref.shape[0]
    patches = sp_ref.shape[0]
    which = lax.broadcasted_iota(jnp.int32, (count, patches), 0)
    wanted = jnp.zeros((count, patches), jnp.int32)
    for i in range(count):
        wanted = jnp.where(which == i, mask_ref[i], wanted)
    onehot = (lax.broadcasted_iota(jnp.int32, (count, patches), 1) == wanted).astype(f32).astype(bf16)
    teacher = unit_rows(dot(onehot, tp_ref[...], NN)).astype(bf16)
    student = unit_rows(dot(onehot, sp_ref[...], NN)).astype(bf16)
    for i in range(rows_ref.shape[0]):
        rows_ref[i, :count] = teacher
        rows_ref[i, count:] = student
    weights_ref[0] = unit_rows(tw_ref[...]).astype(bf16)
    weights_ref[1] = unit_rows(sw_ref[...]).astype(bf16)


def divide_kernel(rows_ref, teacher_ref, student_ref):
    n, both, _ = rows_ref.shape
    count = both // 2
    for i in range(n):
        student_ref[count * i : count * (i + 1)] = rows_ref[i, count:]
        for j in range(teacher_ref.shape[0]):
            teacher_ref[j, count * i : count * (i + 1)] = rows_ref[i, :count]


def first_kernel(rows_ref, weights_ref, expo_ref, column_ref):
    groups, count, _ = rows_ref.shape
    width = weights_ref.shape[2]
    for i in range(weights_ref.shape[0]):
        for j in range(groups):
            score = dot(weights_ref[i, 0], rows_ref[j], NT) * teacher_scale
            expo_ref[width * i : width * (i + 1), count * j : count * (j + 1)] = jnp.exp(score).astype(bf16)
    ones = jnp.ones((1, groups * count), f32)
    spread(column_ref, fold(matvec(ones, expo_ref[...], NT)))


def column_kernel(parts_ref, expo_ref, column_ref):
    row = unfold(1.0 / total_of(parts_ref))
    spread(column_ref, fold(matvec(row, expo_ref[...], NT)))


def row_kernel(parts_ref, expo_ref, out_ref):
    column = unfold(1.0 / total_of(parts_ref))
    spread(out_ref, fold(matvec(column, expo_ref[...], NN)))


def student_kernel(rows_ref, weights_ref, expo_ref, product_ref, total_ref):
    groups, count, _ = rows_ref.shape
    width = weights_ref.shape[2]
    for j in range(groups):
        total = jnp.zeros((1, count), f32)
        for i in range(weights_ref.shape[0]):
            logits = dot(weights_ref[i, 1], rows_ref[j], NT) * student_scale
            total = total + jnp.sum(jnp.exp(logits), axis=0, keepdims=True)
            place = (slice(width * i, width * (i + 1)), slice(count * j, count * (j + 1)))
            product_ref[place] = (expo_ref[place].astype(f32) * logits).astype(bf16)
        per = count // LANES
        total_ref[per * j : per * (j + 1)] = fold(total)


def last_row_kernel(parts_ref, expo_ref, product_ref, total_ref, out_ref):
    column = unfold(1.0 / total_of(parts_ref))
    sums = fold(matvec(column, expo_ref[...], NN))
    cross = fold(matvec(column, product_ref[...], NN))
    spread(out_ref, jnp.concatenate([sums, cross, total_ref[...]], axis=0))


def add_kernel(parts_ref, out_ref):
    spread(out_ref, total_of(parts_ref))


def slope_kernel(parts_ref, column_ref, trows_ref, srows_ref, weights_ref, out_ref):
    groups, count, _ = trows_ref.shape
    n, _, width, depth = weights_ref.shape
    lines = groups * count // LANES
    sums = total_of(parts_ref)
    row = 1.0 / sums[:lines]
    student_total = sums[2 * lines :]
    partial = jnp.sum(jnp.log(student_total)) - jnp.sum(row * sums[lines : 2 * lines])
    row = unfold(row)
    inverse = unfold(1.0 / student_total)
    column = unfold(1.0 / total_of(column_ref))
    column = jnp.broadcast_to(column, (8, n * width)).T[:, 0:1]
    for i in range(n):
        grad = jnp.zeros((width, depth), f32)
        for j in range(groups):
            place = slice(count * j, count * (j + 1))
            target = jnp.exp(dot(weights_ref[i, 0], trows_ref[j], NT) * teacher_scale)
            expo = jnp.exp(dot(weights_ref[i, 1], srows_ref[j], NT) * student_scale)
            target = target * column[width * i : width * (i + 1)] * row[:, place]
            slope = ((expo * inverse[:, place] - target) * student_scale).astype(bf16)
            grad = grad + dot(slope, srows_ref[j], NN)
        out_ref[i, :width] = grad.astype(bf16)
    partial = jnp.full((16, depth), partial, f32)
    high = partial.astype(bf16).astype(f32)
    middle = (partial - high).astype(bf16).astype(f32)
    which = lax.broadcasted_iota(jnp.int32, (16, depth), 0)
    pieces = jnp.where(which == 0, high, jnp.where(which == 1, middle, jnp.where(which == 2, partial - high - middle, 0.0)))
    for i in range(n):
        out_ref[i, width:] = pieces.astype(bf16)


def finish_kernel(rows, parts_ref, proto_ref, loss_ref, grad_ref):
    width = proto_ref.shape[0]
    unit_grad = parts_ref[0, :width].astype(f32)
    pieces = parts_ref[0, width:].astype(f32)
    for i in range(1, parts_ref.shape[0]):
        unit_grad = unit_grad + parts_ref[i, :width].astype(f32)
        pieces = pieces + parts_ref[i, width:].astype(f32)
    loss_ref[...] = jnp.sum(pieces, axis=0, keepdims=True)[:, :LANES] / rows
    proto = proto_ref[...].astype(f32)
    scale = lax.rsqrt(jnp.sum(proto * proto, axis=1, keepdims=True) + norm_eps)
    unit = proto * scale
    grad_ref[...] = (unit_grad - unit * jnp.sum(unit * unit_grad, axis=1, keepdims=True)) * scale


def call(kernel, outs, *args, smem=()):
    vmem = pl.BlockSpec(memory_space=pltpu.VMEM)
    return pl.pallas_call(
        kernel,
        out_shape=outs,
        in_specs=[pl.BlockSpec(memory_space=pltpu.SMEM) if i in smem else vmem for i in range(len(args))],
        out_specs=jax.tree.map(lambda _: vmem, outs),
        compiler_params=pltpu.CompilerParams(vmem_limit_bytes=40 * 1024 * 1024),
    )(*args)


def per_device(nz, ny, nx, nc, student_patches, teacher_patches, mask_rows, student_proto, teacher_proto):
    shape = jax.ShapeDtypeStruct
    count = mask_rows.shape[0]
    width, depth = student_proto.shape
    near = ny * nc
    rows = count * nz * near
    columns = width * nx
    row_lines, column_lines = rows // LANES, columns // LANES

    def exchange(values, axes):
        return lax.all_to_all(values, axes, 0, 0, tiled=True)

    picked, weights = call(
        prepare_kernel,
        (shape((nz, 2 * count, depth), bf16), shape((2, width, depth), bf16)),
        mask_rows, student_patches, teacher_patches, student_proto, teacher_proto, smem=(0,),
    )
    weights = lax.all_gather(weights, "x", axis=0, tiled=False)
    picked = exchange(picked, "z")
    teacher_local, student_local = call(
        divide_kernel,
        (shape((near, nz * count, depth), bf16), shape((nz * count, depth), bf16)),
        picked,
    )
    student_rows = lax.all_gather(student_local, ("y", "c"), axis=0, tiled=False)
    teacher_rows = exchange(teacher_local, ("y", "c"))
    student_rows = student_rows.reshape(teacher_rows.shape)

    column_out = shape((nx, column_lines, LANES), f32)
    expo, column = call(
        first_kernel, (shape((columns, rows), bf16), column_out), teacher_rows, weights
    )
    for step in range(ITERS):
        if step:
            column = call(column_kernel, column_out, row, expo)
        column = exchange(column, "x")
        lines = row_lines
        if step < ITERS - 1:
            row = call(row_kernel, shape((near, lines, LANES), f32), column, expo)
        else:
            product, student_total = call(
                student_kernel, (shape((columns, rows), bf16), shape((lines, LANES), f32)),
                student_rows, weights, expo,
            )
            lines = 3 * row_lines
            row = call(
                last_row_kernel, shape((near, lines, LANES), f32), column, expo, product, student_total
            )
        row = exchange(row, ("y", "c"))
        row = call(add_kernel, shape((nz, lines, LANES), f32), row)
        row = exchange(row, "z")
    grads = call(
        slope_kernel, shape((nx, width + 16, depth), bf16), row, column, teacher_rows, student_rows, weights
    )
    grads = exchange(grads, "x")
    loss, proto_grad = call(
        lambda *refs: finish_kernel(rows * nx, *refs),
        (shape((1, LANES), f32), shape((width, depth), f32)),
        grads, student_proto,
    )
    return (loss[0, 0], proto_grad)


def solution(mesh):
    nz = mesh.shape["grp"]
    ny, nx, nc = 4, 4, 2
    axes = ("z", "y", "x", "c")
    inner = Mesh(mesh.devices.reshape(nz, ny, nx, nc), axes)
    placed = (P(axes, None), P(axes, None), P(axes), P(axes, None), P(axes, None))
    return jax.shard_map(
        lambda *args: per_device(nz, ny, nx, nc, *args),
        mesh=inner,
        in_specs=placed,
        out_specs=(P(), P(axes, None)),
        check_vma=False,
    )
```

```python
import jax
import jax.numpy as jnp
from jax import lax
from jax.experimental import pallas as pl
from jax.experimental.pallas import tpu as pltpu
from jax.sharding import Mesh, PartitionSpec as P

LANES = 128

norm_eps = 1e-06
teacher_scale = 1.0 / 0.07
student_scale = 1.0 / 0.1

f32 = jnp.float32
bf16 = jnp.bfloat16
NT = (((1,), (1,)), ((), ()))
NN = (((1,), (0,)), ((), ()))


def dot(a, b, dims):
    return lax.dot_general(a, b, dims, preferred_element_type=f32)


def unit_rows(values):
    values = values.astype(f32)
    return values * lax.rsqrt(jnp.sum(values * values, axis=1, keepdims=True) + norm_eps)


def fold(row):
    n = row.shape[1] // LANES
    return jnp.concatenate([row[:, LANES * i : LANES * (i + 1)] for i in range(n)], axis=0)


def unfold(tile):
    return jnp.concatenate([tile[i : i + 1, :] for i in range(tile.shape[0])], axis=1)


def split_rows(row):
    high = row.astype(bf16).astype(f32)
    which = lax.broadcasted_iota(jnp.int32, (16, row.shape[1]), 0)
    return jnp.where(which == 0, high, jnp.where(which == 1, row - high, 0.0)).astype(bf16)


def matvec(row, matrix, dims):
    return jnp.sum(dot(split_rows(row), matrix, dims), axis=0, keepdims=True)


def spread(out_ref, tile):
    for i in range(out_ref.shape[0]):
        out_ref[i] = tile


def total_of(parts_ref):
    total = parts_ref[0]
    for i in range(1, parts_ref.shape[0]):
        total = total + parts_ref[i]
    return total


def rows_kernel(mask_ref, sp_ref, tp_ref, rows_ref, mask, sp, tp, sems):
    copies = [
        pltpu.make_async_copy(source, target, sems.at[i])
        for i, (source, target) in enumerate(((mask_ref, mask), (tp_ref, tp), (sp_ref, sp)))
    ]
    for copy in copies:
        copy.start()
    count = mask_ref.shape[0]
    patches = sp_ref.shape[0]
    copies[0].wait()
    which = lax.broadcasted_iota(jnp.int32, (count, patches), 0)
    wanted = jnp.zeros((count, patches), jnp.int32)
    for i in range(count):
        wanted = jnp.where(which == i, mask[i], wanted)
    onehot = (lax.broadcasted_iota(jnp.int32, (count, patches), 1) == wanted).astype(f32).astype(bf16)
    copies[1].wait()
    teacher = unit_rows(dot(onehot, tp[...], NN)).astype(bf16)
    copies[2].wait()
    student = unit_rows(dot(onehot, sp[...], NN)).astype(bf16)
    for i in range(rows_ref.shape[0]):
        rows_ref[i, :count] = teacher
        rows_ref[i, count:] = student


def weights_kernel(tw_ref, sw_ref, weights_ref, tw, sw, sems):
    copies = [
        pltpu.make_async_copy(source, target, sems.at[i])
        for i, (source, target) in enumerate(((tw_ref, tw), (sw_ref, sw)))
    ]
    for copy in copies:
        copy.start()
    copies[0].wait()
    weights_ref[0] = unit_rows(tw[...]).astype(bf16)
    copies[1].wait()
    weights_ref[1] = unit_rows(sw[...]).astype(bf16)


def divide_kernel(rows_ref, teacher_ref, student_ref):
    n, both, _ = rows_ref.shape
    count = both // 2
    for i in range(n):
        student_ref[count * i : count * (i + 1)] = rows_ref[i, count:]
        for j in range(teacher_ref.shape[0]):
            teacher_ref[j, count * i : count * (i + 1)] = rows_ref[i, :count]


def first_kernel(rows_ref, weights_ref, expo_ref, column_ref):
    groups, count, _ = rows_ref.shape
    width = weights_ref.shape[2]
    for i in range(weights_ref.shape[0]):
        for j in range(groups):
            score = dot(weights_ref[i, 0], rows_ref[j], NT) * teacher_scale
            expo_ref[width * i : width * (i + 1), count * j : count * (j + 1)] = jnp.exp(score).astype(bf16)
    ones = jnp.ones((1, groups * count), f32)
    spread(column_ref, fold(matvec(ones, expo_ref[...], NT)))


def column_kernel(parts_ref, expo_ref, column_ref):
    row = unfold(1.0 / total_of(parts_ref))
    spread(column_ref, fold(matvec(row, expo_ref[...], NT)))


def row_kernel(parts_ref, expo_ref, out_ref):
    column = unfold(1.0 / total_of(parts_ref))
    spread(out_ref, fold(matvec(column, expo_ref[...], NN)))


def load_kernel(gathered_ref, out_ref, sem):
    copy = pltpu.make_async_copy(gathered_ref, out_ref, sem.at[0])
    copy.start()
    copy.wait()


def student_kernel(rows_ref, weights_ref, expo_ref, total_ref, rows_t_ref, weights_t_ref):
    groups, count, _ = rows_ref.shape
    width = weights_ref.shape[2]
    for j in range(groups):
        lanes = slice(count * j, count * (j + 1))
        rows_t_ref[:, lanes] = rows_ref[j].astype(f32).T.astype(bf16)
        total = jnp.zeros((1, count), f32)
        for i in range(weights_ref.shape[0]):
            expo = jnp.exp(dot(weights_ref[i, 1], rows_ref[j], NT) * student_scale)
            total = total + jnp.sum(expo, axis=0, keepdims=True)
            expo_ref[width * i : width * (i + 1), lanes] = expo.astype(bf16)
        per = count // LANES
        total_ref[per * j : per * (j + 1)] = fold(total)
    for i in range(weights_ref.shape[0]):
        weights_t_ref[:, width * i : width * (i + 1)] = weights_ref[i, 1].astype(f32).T.astype(bf16)


def second_row_kernel(parts_ref, expo_ref, total_ref, out_ref, kept_ref, sems):
    pieces = sems.shape[0]
    height = expo_ref.shape[0] // pieces
    copies = [
        pltpu.make_async_copy(expo_ref.at[pl.ds(height * i, height)], kept_ref.at[pl.ds(height * i, height)], sems.at[i])
        for i in range(pieces)
    ]
    for copy in copies:
        copy.start()
    column = unfold(1.0 / total_of(parts_ref))
    sums = jnp.zeros((1, expo_ref.shape[1]), f32)
    for i in range(pieces):
        copies[i].wait()
        place = slice(height * i, height * (i + 1))
        sums = sums + matvec(column[:, place], kept_ref[place], NN)
    spread(out_ref, jnp.concatenate([fold(sums), total_ref[...]], axis=0))


def last_row_kernel(parts_ref, expo_ref, rows_t_ref, weights_t_ref, out_ref):
    column = unfold(1.0 / total_of(parts_ref))
    weighted = (weights_t_ref[...].astype(f32) * column).astype(bf16)
    both = dot(jnp.concatenate([split_rows(column), weighted], axis=0), expo_ref[...], NN)
    sums = jnp.sum(both[:16], axis=0, keepdims=True)
    cross = jnp.sum(both[16:] * rows_t_ref[...].astype(f32), axis=0, keepdims=True) * student_scale
    spread(out_ref, jnp.concatenate([fold(sums), fold(cross)], axis=0))


def add_kernel(parts_ref, out_ref):
    spread(out_ref, total_of(parts_ref))


def add_two_kernel(parts_ref, out_ref):
    total = total_of(parts_ref)
    lines = total.shape[0] // 2
    sums = total[:lines]
    high = sums.astype(bf16)
    spread(out_ref, jnp.concatenate([high, (sums - high.astype(f32)).astype(bf16), total[lines:].astype(bf16)], axis=0))


def halves_of(parts_ref):
    total = parts_ref[0].astype(f32)
    for i in range(1, parts_ref.shape[0]):
        total = total + parts_ref[i].astype(f32)
    lines = total.shape[0] // 3
    return total[:lines] + total[lines : 2 * lines], total[2 * lines :]


def third_column_kernel(parts_ref, expo_ref, column_ref, total_ref):
    sums, total = halves_of(parts_ref)
    spread(column_ref, fold(matvec(unfold(1.0 / sums), expo_ref[...], NT)))
    total_ref[...] = total


def slope_kernel(parts_ref, column_ref, total_ref, target_ref, expo_ref, srows_ref, out_ref, expo, sems):
    groups, count, depth = srows_ref.shape
    n = out_ref.shape[0]
    width = target_ref.shape[0] // n
    copies = [
        pltpu.make_async_copy(expo_ref.at[pl.ds(width * i, width)], expo.at[pl.ds(width * i, width)], sems.at[i])
        for i in range(n)
    ]
    for copy in copies:
        copy.start()
    sums, cross = halves_of(parts_ref)
    row = 1.0 / sums
    student_total = total_ref[...]
    partial = jnp.sum(jnp.log(student_total)) - jnp.sum(row * cross)
    row = unfold(row * student_scale)
    inverse = unfold(student_scale / student_total)
    column = unfold(1.0 / total_of(column_ref))
    column = jnp.broadcast_to(column, (8, n * width)).T[:, 0:1]
    for i in range(n):
        copies[i].wait()
        grad = jnp.zeros((width, depth), f32)
        for j in range(groups):
            lanes = slice(count * j, count * (j + 1))
            place = (slice(width * i, width * (i + 1)), lanes)
            target = target_ref[place].astype(f32) * column[width * i : width * (i + 1)] * row[:, lanes]
            slope = (expo[place].astype(f32) * inverse[:, lanes] - target).astype(bf16)
            grad = grad + dot(slope, srows_ref[j], NN)
        out_ref[i, :width] = grad.astype(bf16)
    partial = jnp.full((16, depth), partial, f32)
    high = partial.astype(bf16).astype(f32)
    middle = (partial - high).astype(bf16).astype(f32)
    which = lax.broadcasted_iota(jnp.int32, (16, depth), 0)
    pieces = jnp.where(which == 0, high, jnp.where(which == 1, middle, jnp.where(which == 2, partial - high - middle, 0.0)))
    for i in range(n):
        out_ref[i, width:] = pieces.astype(bf16)


def finish_kernel(rows, parts_ref, proto_ref, loss_ref, grad_ref):
    width = proto_ref.shape[0]
    unit_grad = parts_ref[0, :width].astype(f32)
    pieces = parts_ref[0, width:].astype(f32)
    for i in range(1, parts_ref.shape[0]):
        unit_grad = unit_grad + parts_ref[i, :width].astype(f32)
        pieces = pieces + parts_ref[i, width:].astype(f32)
    loss_ref[...] = jnp.sum(pieces, axis=0, keepdims=True)[:, :LANES] / rows
    proto = proto_ref[...].astype(f32)
    scale = lax.rsqrt(jnp.sum(proto * proto, axis=1, keepdims=True) + norm_eps)
    unit = proto * scale
    grad_ref[...] = (unit_grad - unit * jnp.sum(unit * unit_grad, axis=1, keepdims=True)) * scale


def call(kernel, outs, *args, place=None, scratch=(), limit=20):
    vmem = pl.BlockSpec(memory_space=pltpu.VMEM)
    place = place or {}
    return pl.pallas_call(
        kernel,
        out_shape=outs,
        in_specs=[pl.BlockSpec(memory_space=place[i]) if i in place else vmem for i in range(len(args))],
        out_specs=jax.tree.map(lambda _: vmem, outs),
        scratch_shapes=scratch,
        compiler_params=pltpu.CompilerParams(vmem_limit_bytes=limit * 1024 * 1024),
    )(*args)


def per_device(nz, ny, nx, nc, student_patches, teacher_patches, mask_rows, student_proto, teacher_proto):
    shape = jax.ShapeDtypeStruct
    held = pltpu.VMEM
    count = mask_rows.shape[0]
    patches = student_patches.shape
    width, depth = student_proto.shape
    near = ny * nc
    rows = count * nz * near
    columns = width * nx
    lines, column_lines = rows // LANES, columns // LANES

    def exchange(values, axes):
        return lax.all_to_all(values, axes, 0, 0, tiled=True)

    def far(values):
        return pltpu.with_memory_space_constraint(values, pltpu.HBM)

    def sems(n):
        return pltpu.SemaphoreType.DMA((n,))

    picked = call(
        rows_kernel,
        shape((nz, 2 * count, depth), bf16),
        far(mask_rows), far(student_patches), far(teacher_patches),
        place={0: pltpu.HBM, 1: pltpu.HBM, 2: pltpu.HBM},
        scratch=[pltpu.SMEM((count,), jnp.int32), pltpu.VMEM(patches, bf16), pltpu.VMEM(patches, bf16), sems(3)],
    )
    late_teacher, late_student, picked = lax.optimization_barrier((teacher_proto, student_proto, picked))
    weights = call(
        weights_kernel,
        shape((2, width, depth), bf16),
        far(late_teacher), far(late_student),
        place={0: pltpu.HBM, 1: pltpu.HBM},
        scratch=[pltpu.VMEM((width, depth), bf16), pltpu.VMEM((width, depth), bf16), sems(2)],
    )
    weights = lax.all_gather(weights, "x", axis=0, tiled=False)
    picked = exchange(picked, "z")
    teacher_local, student_local = call(
        divide_kernel,
        (shape((near, nz * count, depth), bf16), shape((nz * count, depth), bf16)),
        picked,
    )
    weights = call(
        load_kernel, held(weights.shape, bf16), far(weights), place={0: pltpu.HBM}, scratch=[sems(1)]
    )
    student_rows = lax.all_gather(student_local, ("y", "c"), axis=0, tiled=False)
    teacher_rows = exchange(teacher_local, ("y", "c"))
    student_rows = student_rows.reshape(teacher_rows.shape)

    column_out = shape((nx, column_lines, LANES), f32)
    expo, column = call(
        first_kernel, (held((columns, rows), bf16), column_out), teacher_rows, weights
    )
    column = exchange(column, "x")
    row = call(row_kernel, shape((near, lines, LANES), f32), column, expo)
    row = exchange(row, ("y", "c"))
    row = call(add_kernel, shape((nz, lines, LANES), f32), row)
    row = exchange(row, "z")

    column = call(column_kernel, column_out, row, expo)
    student_rows, column = lax.optimization_barrier((student_rows, column))
    student_expo, student_total, rows_t, weights_t = call(
        student_kernel,
        (shape((columns, rows), bf16), shape((lines, LANES), f32), shape((depth, rows), bf16), shape((depth, columns), bf16)),
        student_rows, weights,
    )
    column = exchange(column, "x")
    row, expo = call(
        second_row_kernel,
        (shape((near, 2 * lines, LANES), f32), held((columns, rows), bf16)),
        column, far(expo), student_total,
        place={1: pltpu.HBM},
        scratch=[sems(4)],
    )
    row = exchange(row, ("y", "c"))
    row = call(add_two_kernel, shape((nz, 3 * lines, LANES), bf16), row)
    row = exchange(row, "z")

    column, student_total = call(third_column_kernel, (column_out, shape((lines, LANES), f32)), row, expo)
    column = exchange(column, "x")
    row = call(last_row_kernel, shape((near, 2 * lines, LANES), f32), column, expo, rows_t, weights_t)
    row = exchange(row, ("y", "c"))
    row = call(add_two_kernel, shape((nz, 3 * lines, LANES), bf16), row)
    row = exchange(row, "z")

    grads = call(
        slope_kernel,
        shape((nx, width + 16, depth), bf16),
        row, column, student_total, expo, far(student_expo), student_rows,
        place={4: pltpu.HBM},
        scratch=[pltpu.VMEM((columns, rows), bf16), sems(nx)],
    )
    grads = exchange(grads, "x")
    loss, proto_grad = call(
        lambda *refs: finish_kernel(rows * nx, *refs),
        (shape((1, LANES), f32), shape((width, depth), f32)),
        grads, student_proto,
    )
    return (loss[0, 0], proto_grad)


def solution(mesh):
    nz = mesh.shape["grp"]
    ny, nx, nc = 4, 4, 2
    axes = ("z", "y", "x", "c")
    inner = Mesh(mesh.devices.reshape(nz, ny, nx, nc), axes)
    placed = (P(axes, None), P(axes, None), P(axes), P(axes, None), P(axes, None))
    return jax.shard_map(
        lambda *args: per_device(nz, ny, nx, nc, *args),
        mesh=inner,
        in_specs=placed,
        out_specs=(P(), P(axes, None)),
        check_vma=False,
    )
```

```python
import jax
import jax.numpy as jnp
from jax import lax
from jax.experimental import pallas as pl
from jax.experimental.pallas import tpu as pltpu
from jax.sharding import Mesh, PartitionSpec as P

LANES = 128

norm_eps = 1e-06
teacher_scale = 1.0 / 0.07
student_scale = 1.0 / 0.1

f32 = jnp.float32
bf16 = jnp.bfloat16
NT = (((1,), (1,)), ((), ()))
NN = (((1,), (0,)), ((), ()))


def dot(a, b, dims):
    return lax.dot_general(a, b, dims, preferred_element_type=f32)


def unit_rows(values):
    values = values.astype(f32)
    return values * lax.rsqrt(jnp.sum(values * values, axis=1, keepdims=True) + norm_eps)


def fold(row):
    n = row.shape[1] // LANES
    return jnp.concatenate([row[:, LANES * i : LANES * (i + 1)] for i in range(n)], axis=0)


def unfold(tile):
    return jnp.concatenate([tile[i : i + 1, :] for i in range(tile.shape[0])], axis=1)


def split_rows(row):
    high = row.astype(bf16).astype(f32)
    which = lax.broadcasted_iota(jnp.int32, (16, row.shape[1]), 0)
    return jnp.where(which == 0, high, jnp.where(which == 1, row - high, 0.0)).astype(bf16)


def matvec(row, matrix, dims):
    return jnp.sum(dot(split_rows(row), matrix, dims), axis=0, keepdims=True)


def spread(out_ref, tile):
    for i in range(out_ref.shape[0]):
        out_ref[i] = tile


def total_of(parts_ref):
    total = parts_ref[0]
    for i in range(1, parts_ref.shape[0]):
        total = total + parts_ref[i]
    return total


def rows_kernel(mask_ref, sp_ref, tp_ref, rows_ref, mask, sp, tp, sems):
    copies = [
        pltpu.make_async_copy(source, target, sems.at[i])
        for i, (source, target) in enumerate(((mask_ref, mask), (tp_ref, tp), (sp_ref, sp)))
    ]
    for copy in copies:
        copy.start()
    count = mask_ref.shape[0]
    patches = sp_ref.shape[0]
    copies[0].wait()
    which = lax.broadcasted_iota(jnp.int32, (count, patches), 0)
    wanted = jnp.zeros((count, patches), jnp.int32)
    for i in range(count):
        wanted = jnp.where(which == i, mask[i], wanted)
    onehot = (lax.broadcasted_iota(jnp.int32, (count, patches), 1) == wanted).astype(f32).astype(bf16)
    copies[1].wait()
    teacher = unit_rows(dot(onehot, tp[...], NN)).astype(bf16)
    copies[2].wait()
    student = unit_rows(dot(onehot, sp[...], NN)).astype(bf16)
    for i in range(rows_ref.shape[0]):
        rows_ref[i, :count] = teacher
        rows_ref[i, count:] = student


def weights_kernel(tw_ref, sw_ref, weights_ref, tw, sw, sems):
    copies = [
        pltpu.make_async_copy(source, target, sems.at[i])
        for i, (source, target) in enumerate(((tw_ref, tw), (sw_ref, sw)))
    ]
    for copy in copies:
        copy.start()
    copies[0].wait()
    weights_ref[0] = unit_rows(tw[...]).astype(bf16)
    copies[1].wait()
    weights_ref[1] = unit_rows(sw[...]).astype(bf16)


def divide_kernel(rows_ref, out_ref):
    n, both, _ = rows_ref.shape
    count = both // 2
    for i in range(n):
        for j in range(out_ref.shape[0]):
            out_ref[j, count * i : count * (i + 1)] = rows_ref[i, :count]
            out_ref[j, count * (n + i) : count * (n + i + 1)] = rows_ref[i, count:]


def stack_kernel(*refs):
    *parts, out_ref, sems = refs
    copies = [pltpu.make_async_copy(part, out_ref.at[i], sems.at[i]) for i, part in enumerate(parts)]
    for copy in copies:
        copy.start()
    for copy in copies:
        copy.wait()


def pair_kernel(place_ref, *refs):
    *parts, other_ref, out_ref, sems = refs
    n = len(parts)
    core = place_ref[n]
    copies = []
    for i, part in enumerate(parts):
        copies.append(pltpu.make_async_copy(part, out_ref.at[place_ref[i], core], sems.at[0, i]))
        copies.append(pltpu.make_async_copy(other_ref.at[i], out_ref.at[place_ref[i], 1 - core], sems.at[1, i]))
    for copy in copies:
        copy.start()
    for copy in copies:
        copy.wait()


def first_kernel(rows_ref, weights_ref, target_ref, expo_ref, product_ref, total_ref, column_ref):
    groups, both, _ = rows_ref.shape
    count = both // 2
    nx, nc, _, width, _ = weights_ref.shape
    for j in range(groups):
        total = jnp.zeros((1, count), f32)
        for i in range(nx * nc):
            place = (slice(width * i, width * (i + 1)), slice(count * j, count * (j + 1)))
            weights = weights_ref.at[i // nc, i % nc]
            target = jnp.exp(dot(weights[0], rows_ref[j, :count], NT) * teacher_scale)
            logits = dot(weights[1], rows_ref[j, count:], NT) * student_scale
            expo = jnp.exp(logits)
            total = total + jnp.sum(expo, axis=0, keepdims=True)
            target_ref[place] = target.astype(bf16)
            expo_ref[place] = expo.astype(bf16)
            product_ref[place] = (target * logits).astype(bf16)
        per = count // LANES
        total_ref[per * j : per * (j + 1)] = fold(total)
    ones = jnp.ones((1, groups * count), f32)
    spread(column_ref, fold(matvec(ones, target_ref[...], NT)))


def column_kernel(parts_ref, expo_ref, column_ref):
    row = unfold(1.0 / total_of(parts_ref))
    spread(column_ref, fold(matvec(row, expo_ref[...], NT)))


def row_kernel(parts_ref, expo_ref, out_ref):
    column = unfold(1.0 / total_of(parts_ref))
    spread(out_ref, fold(matvec(column, expo_ref[...], NN)))


def second_row_kernel(parts_ref, expo_ref, total_ref, out_ref):
    column = unfold(1.0 / total_of(parts_ref))
    sums = fold(matvec(column, expo_ref[...], NN))
    spread(out_ref, jnp.concatenate([sums, total_ref[...]], axis=0))


def last_row_kernel(parts_ref, expo_ref, product_ref, out_ref):
    column = unfold(1.0 / total_of(parts_ref))
    sums = fold(matvec(column, expo_ref[...], NN))
    cross = fold(matvec(column, product_ref[...], NN))
    spread(out_ref, jnp.concatenate([sums, cross], axis=0))


def add_kernel(parts_ref, out_ref):
    spread(out_ref, total_of(parts_ref))


def third_column_kernel(parts_ref, expo_ref, column_ref, total_ref):
    both = total_of(parts_ref)
    lines = both.shape[0] // 2
    spread(column_ref, fold(matvec(unfold(1.0 / both[:lines]), expo_ref[...], NT)))
    total_ref[...] = both[lines:]


def pieces_of(row):
    high = row.astype(bf16).astype(f32)
    middle = (row - high).astype(bf16).astype(f32)
    which = lax.broadcasted_iota(jnp.int32, (16, row.shape[1]), 0)
    pieces = jnp.where(which == 0, high, jnp.where(which == 1, middle, jnp.where(which == 2, row - high - middle, 0.0)))
    return pieces.astype(bf16)


def slope_kernel(core_ref, parts_ref, column_ref, total_ref, target_ref, expo_ref, rows_ref, out_ref, columns):
    groups, both, depth = rows_ref.shape
    count = both // 2
    n, width, _ = out_ref.shape
    width = width - 16
    nc = target_ref.shape[0] // (n * width)
    core = core_ref[0]
    per = width // LANES
    columns[...] = 1.0 / total_of(column_ref)
    sums = total_of(parts_ref)
    lines = sums.shape[0] // 2
    row = 1.0 / sums[:lines]
    student_total = total_ref[...]
    partial = jnp.sum(jnp.log(student_total)) - jnp.sum(row * sums[lines:])
    row = unfold(row * student_scale)
    inverse = unfold(student_scale / student_total)
    for i in range(n):
        block = i * nc + core
        column = jnp.concatenate([columns[pl.ds(block * per + k, 1), :] for k in range(per)], axis=1)
        column = jnp.broadcast_to(column, (8, width)).T[:, 0:1]
        start = pl.multiple_of(block * width, width)
        grad = jnp.zeros((width, depth), f32)
        for j in range(groups):
            lanes = slice(count * j, count * (j + 1))
            target = target_ref[pl.ds(start, width), lanes].astype(f32) * column * row[:, lanes]
            slope = (expo_ref[pl.ds(start, width), lanes].astype(f32) * inverse[:, lanes] - target).astype(bf16)
            grad = grad + dot(slope, rows_ref[j, count:], NN)
        out_ref[i, :width] = grad.astype(out_ref.dtype)
        out_ref[i, width:] = pieces_of(jnp.full((1, depth), partial, f32)).astype(out_ref.dtype)


def join_kernel(own_ref, other_ref, out_ref):
    width = own_ref.shape[1] - 16
    for i in range(own_ref.shape[0]):
        out_ref[i, :width] = (own_ref[i, :width] + other_ref[i, :width].astype(f32)).astype(bf16)
        pieces = own_ref[i, width:] + other_ref[i, width:].astype(f32)
        out_ref[i, width:] = pieces_of(jnp.sum(pieces, axis=0, keepdims=True))


def finish_kernel(rows, parts_ref, proto_ref, loss_ref, grad_ref):
    width = proto_ref.shape[0]
    unit_grad = parts_ref[0, :width].astype(f32)
    pieces = parts_ref[0, width:].astype(f32)
    for i in range(1, parts_ref.shape[0]):
        unit_grad = unit_grad + parts_ref[i, :width].astype(f32)
        pieces = pieces + parts_ref[i, width:].astype(f32)
    loss_ref[...] = jnp.sum(pieces, axis=0, keepdims=True)[:, :LANES] / rows
    proto = proto_ref[...].astype(f32)
    scale = lax.rsqrt(jnp.sum(proto * proto, axis=1, keepdims=True) + norm_eps)
    unit = proto * scale
    grad_ref[...] = (unit_grad - unit * jnp.sum(unit * unit_grad, axis=1, keepdims=True)) * scale


def call(kernel, outs, *args, place=None, scratch=(), limit=20):
    vmem = pl.BlockSpec(memory_space=pltpu.VMEM)
    place = place or {}
    return pl.pallas_call(
        kernel,
        out_shape=outs,
        in_specs=[pl.BlockSpec(memory_space=place[i]) if i in place else vmem for i in range(len(args))],
        out_specs=jax.tree.map(lambda _: vmem, outs),
        scratch_shapes=scratch,
        compiler_params=pltpu.CompilerParams(vmem_limit_bytes=limit * 1024 * 1024),
    )(*args)


def per_device(nz, ny, nx, nc, student_patches, teacher_patches, mask_rows, student_proto, teacher_proto):
    shape = jax.ShapeDtypeStruct
    held = pltpu.VMEM
    count = mask_rows.shape[0]
    patches = student_patches.shape
    width, depth = student_proto.shape
    rows = count * nz * ny
    columns = width * nx * nc
    lines, column_lines = rows // LANES, columns // LANES

    def exchange(values, axes):
        return lax.all_to_all(values, axes, 0, 0, tiled=True)

    def far(values):
        return pltpu.with_memory_space_constraint(values, pltpu.HBM)

    def sems(n):
        return pltpu.SemaphoreType.DMA((n,))

    picked = call(
        rows_kernel,
        shape((nz, 2 * count, depth), bf16),
        far(mask_rows), far(student_patches), far(teacher_patches),
        place={0: pltpu.HBM, 1: pltpu.HBM, 2: pltpu.HBM},
        scratch=[pltpu.SMEM((count,), jnp.int32), pltpu.VMEM(patches, bf16), pltpu.VMEM(patches, bf16), sems(3)],
    )
    late_teacher, late_student, picked = lax.optimization_barrier((teacher_proto, student_proto, picked))
    weights = call(
        weights_kernel,
        shape((2, width, depth), bf16),
        far(late_teacher), far(late_student),
        place={0: pltpu.HBM, 1: pltpu.HBM},
        scratch=[pltpu.VMEM((width, depth), bf16), pltpu.VMEM((width, depth), bf16), sems(2)],
    )
    parts = [weights] + [lax.ppermute(weights, "x", [(i, (i + k) % nx) for i in range(nx)]) for k in range(1, nx)]
    core = lax.axis_index("c").astype(jnp.int32).reshape(1)
    places = (lax.axis_index("x") - jnp.arange(nx, dtype=jnp.int32)) % nx
    places, core, other_core, picked = lax.optimization_barrier(
        (jnp.concatenate([places, core]), core, nc - 1 - core, picked)
    )
    picked = exchange(picked, "z")
    picked, parts[0] = lax.optimization_barrier((picked, parts[0]))
    picked = call(divide_kernel, shape((ny, 2 * nz * count, depth), bf16), picked)
    picked, *parts[1:] = lax.optimization_barrier((picked, *parts[1:]))
    parts = [far(part) for part in parts]
    stacked = call(
        stack_kernel,
        shape((nx, *weights.shape), bf16),
        *parts,
        place={i: pltpu.HBM for i in range(nx)},
        scratch=[sems(nx)],
    )
    other = lax.ppermute(stacked, "c", [(i, (i + 1) % nc) for i in range(nc)])
    weights = call(
        pair_kernel,
        held((nx, nc, *weights.shape), bf16),
        places, *parts, far(other),
        place={0: pltpu.SMEM, **{1 + i: pltpu.HBM for i in range(nx + 1)}},
        scratch=[pltpu.SemaphoreType.DMA((nc, nx))],
    )
    picked = exchange(picked, "y")

    column_out = shape((nx * nc, column_lines, LANES), f32)
    row_out = shape((ny, lines, LANES), f32)
    rows_out = shape((ny, 2 * lines, LANES), f32)
    matrix = held((columns, rows), bf16)
    target, expo, product, student_total, column = call(
        first_kernel, (matrix, matrix, matrix, shape((lines, LANES), f32), column_out), picked, weights
    )
    column = exchange(column, ("x", "c"))
    row = call(row_kernel, row_out, column, target)
    row = exchange(row, "y")
    row = call(add_kernel, shape((nz, lines, LANES), f32), row)
    row = exchange(row, "z")

    column = call(column_kernel, column_out, row, target)
    column = exchange(column, ("x", "c"))
    row = call(second_row_kernel, rows_out, column, target, student_total)
    row = exchange(row, "y")
    row = call(add_kernel, shape((nz, 2 * lines, LANES), f32), row)
    row = exchange(row, "z")

    column, student_total = call(third_column_kernel, (column_out, shape((lines, LANES), f32)), row, target)
    column = exchange(column, ("x", "c"))
    row = call(last_row_kernel, rows_out, column, target, product)
    row = exchange(row, "y")
    row = call(add_kernel, shape((nz, 2 * lines, LANES), f32), row)
    row = exchange(row, "z")

    halves = []
    for which, kind in ((other_core, bf16), (core, f32)):
        halves.append(
            call(
                slope_kernel,
                shape((nx, width + 16, depth), kind),
                which, row, column, student_total, target, expo, picked,
                place={0: pltpu.SMEM},
                scratch=[pltpu.VMEM((column_lines, LANES), f32)],
            )
        )
    other = lax.ppermute(halves[0], "c", [(i, (i + 1) % nc) for i in range(nc)])
    grads = call(join_kernel, shape((nx, width + 16, depth), bf16), halves[1], other)
    grads = exchange(grads, "x")
    loss, proto_grad = call(
        lambda *refs: finish_kernel(rows * nx * nc, *refs),
        (shape((1, LANES), f32), shape((width, depth), f32)),
        grads, student_proto,
    )
    return (loss[0, 0], proto_grad)


def solution(mesh):
    nz = mesh.shape["grp"]
    ny, nx, nc = 4, 4, 2
    axes = ("z", "y", "x", "c")
    inner = Mesh(mesh.devices.reshape(nz, ny, nx, nc), axes)
    placed = (P(axes, None), P(axes, None), P(axes), P(axes, None), P(axes, None))
    return jax.shard_map(
        lambda *args: per_device(nz, ny, nx, nc, *args),
        mesh=inner,
        in_specs=placed,
        out_specs=(P(), P(axes, None)),
        check_vma=False,
    )
```

```python
import functools

import jax
import jax.numpy as jnp
from jax import lax
from jax.experimental import pallas as pl
from jax.experimental.pallas import tpu as pltpu
from jax.sharding import Mesh, PartitionSpec as P

LANES = 128

norm_eps = 1e-06
teacher_scale = 1.0 / 0.07
student_scale = 1.0 / 0.1
log2_e = 1.4426950408889634

f32 = jnp.float32
bf16 = jnp.bfloat16
NT = (((1,), (1,)), ((), ()))
NN = (((1,), (0,)), ((), ()))


def dot(a, b, dims):
    return lax.dot_general(a, b, dims, preferred_element_type=f32)


def unit_rows(values):
    values = values.astype(f32)
    return values * lax.rsqrt(jnp.sum(values * values, axis=1, keepdims=True) + norm_eps)


def fold(row):
    n = row.shape[1] // LANES
    return jnp.concatenate([row[:, LANES * i : LANES * (i + 1)] for i in range(n)], axis=0)


def unfold(tile):
    return jnp.concatenate([tile[i : i + 1, :] for i in range(tile.shape[0])], axis=1)


def split_rows(row):
    high = row.astype(bf16).astype(f32)
    which = lax.broadcasted_iota(jnp.int32, (16, row.shape[1]), 0)
    return jnp.where(which == 0, high, jnp.where(which == 1, row - high, 0.0)).astype(bf16)


def matvec(row, matrix, dims):
    return jnp.sum(dot(split_rows(row), matrix, dims), axis=0, keepdims=True)


def spread(out_ref, tile):
    for i in range(out_ref.shape[0]):
        out_ref[i] = tile


def total_of(parts_ref):
    total = parts_ref[0]
    for i in range(1, parts_ref.shape[0]):
        total = total + parts_ref[i]
    return total


def rows_kernel(mask_ref, sp_ref, tp_ref, rows_ref, mask, sp, tp, sems):
    copies = [
        pltpu.make_async_copy(source, target, sems.at[i])
        for i, (source, target) in enumerate(((mask_ref, mask), (tp_ref, tp), (sp_ref, sp)))
    ]
    for copy in copies:
        copy.start()
    count = mask_ref.shape[0]
    patches = sp_ref.shape[0]
    copies[0].wait()
    which = lax.broadcasted_iota(jnp.int32, (count, patches), 0)
    wanted = jnp.zeros((count, patches), jnp.int32)
    for i in range(count):
        wanted = jnp.where(which == i, mask[i], wanted)
    onehot = (lax.broadcasted_iota(jnp.int32, (count, patches), 1) == wanted).astype(f32).astype(bf16)
    copies[1].wait()
    teacher = unit_rows(dot(onehot, tp[...], NN)).astype(bf16)
    copies[2].wait()
    student = unit_rows(dot(onehot, sp[...], NN)).astype(bf16)
    for i in range(rows_ref.shape[0]):
        rows_ref[i, :count] = teacher
        rows_ref[i, count:] = student


def weights_kernel(tw_ref, sw_ref, weights_ref, tw, sw, sems):
    copies = [
        pltpu.make_async_copy(source, target, sems.at[i])
        for i, (source, target) in enumerate(((tw_ref, tw), (sw_ref, sw)))
    ]
    for copy in copies:
        copy.start()
    copies[0].wait()
    weights_ref[0] = unit_rows(tw[...]).astype(bf16)
    copies[1].wait()
    weights_ref[1] = unit_rows(sw[...]).astype(bf16)


def divide_kernel(rows_ref, out_ref):
    n, both, _ = rows_ref.shape
    count = both // 2
    for i in range(n):
        for j in range(out_ref.shape[0]):
            out_ref[j, count * i : count * (i + 1)] = rows_ref[i, :count]
            out_ref[j, count * (n + i) : count * (n + i + 1)] = rows_ref[i, count:]


def place_kernel(place_ref, *refs):
    *parts, out_ref, sems = refs
    copies = [
        pltpu.make_async_copy(part, out_ref.at[place_ref[i]], sems.at[i]) for i, part in enumerate(parts)
    ]
    for copy in copies:
        copy.start()
    for copy in copies:
        copy.wait()


def half_kernel(rows_ref, weights_ref, target_ref, expo_ref, product_ref, total_ref, sums_ref):
    groups, both, _ = rows_ref.shape
    count = both // 2
    nx, _, width, _ = weights_ref.shape
    for j in range(groups):
        total = jnp.zeros((1, count), f32)
        for i in range(nx):
            place = (slice(width * i, width * (i + 1)), slice(count * j, count * (j + 1)))
            target = jnp.exp2(dot(weights_ref[i, 0], rows_ref[j, :count], NT) * (teacher_scale * log2_e))
            score = dot(weights_ref[i, 1], rows_ref[j, count:], NT)
            expo = jnp.exp2(score * (student_scale * log2_e))
            total = total + jnp.sum(expo, axis=0, keepdims=True)
            target_ref[place] = target.astype(bf16)
            expo_ref[place] = expo.astype(bf16)
            product_ref[place] = (target * score).astype(bf16)
        per = count // LANES
        total_ref[per * j : per * (j + 1)] = fold(total)
    sums_ref[...] = fold(matvec(jnp.ones((1, groups * count), f32), target_ref[...], NT))


def spread_halves(core_ref, out_ref, own, other):
    core = core_ref[0]
    lines = own.shape[0]
    for i in range(out_ref.shape[0]):
        out_ref[i, pl.ds(pl.multiple_of(core * lines, lines), lines)] = own
        out_ref[i, pl.ds(pl.multiple_of((1 - core) * lines, lines), lines)] = other


def half_columns(core_ref, parts_ref, columns):
    columns[...] = 1.0 / total_of(parts_ref)
    core = core_ref[0]
    lines = columns.shape[0] // 2
    own = columns[pl.ds(pl.multiple_of(core * lines, lines), lines), :]
    other = columns[pl.ds(pl.multiple_of((1 - core) * lines, lines), lines), :]
    return unfold(own), unfold(other)


def join_first_kernel(core_ref, own_ref, other_ref, column_ref):
    spread_halves(core_ref, column_ref, own_ref[...], other_ref[...])


def column_kernel(core_ref, parts_ref, own_ref, other_ref, column_ref):
    row = unfold(1.0 / total_of(parts_ref))
    spread_halves(core_ref, column_ref, fold(matvec(row, own_ref[...], NT)), fold(matvec(row, other_ref[...], NT)))


def third_column_kernel(core_ref, parts_ref, own_ref, other_ref, column_ref, total_ref):
    both = total_of(parts_ref)
    lines = both.shape[0] // 2
    row = unfold(1.0 / both[:lines])
    spread_halves(core_ref, column_ref, fold(matvec(row, own_ref[...], NT)), fold(matvec(row, other_ref[...], NT)))
    total_ref[...] = both[lines:]


def row_kernel(core_ref, parts_ref, own_ref, other_ref, out_ref, columns):
    own, other = half_columns(core_ref, parts_ref, columns)
    spread(out_ref, fold(matvec(own, own_ref[...], NN) + matvec(other, other_ref[...], NN)))


def second_row_kernel(core_ref, parts_ref, own_ref, other_ref, own_total_ref, other_total_ref, out_ref, columns):
    own, other = half_columns(core_ref, parts_ref, columns)
    sums = fold(matvec(own, own_ref[...], NN) + matvec(other, other_ref[...], NN))
    spread(out_ref, jnp.concatenate([sums, own_total_ref[...] + other_total_ref[...]], axis=0))


def last_row_kernel(core_ref, parts_ref, own_ref, other_ref, own_product_ref, other_product_ref, out_ref, columns):
    own, other = half_columns(core_ref, parts_ref, columns)
    sums = fold(matvec(own, own_ref[...], NN) + matvec(other, other_ref[...], NN))
    cross = fold(matvec(own, own_product_ref[...], NN) + matvec(other, other_product_ref[...], NN)) * student_scale
    spread(out_ref, jnp.concatenate([sums, cross], axis=0))


def add_kernel(parts_ref, out_ref):
    spread(out_ref, total_of(parts_ref))


def pieces_of(row):
    high = row.astype(bf16).astype(f32)
    middle = (row - high).astype(bf16).astype(f32)
    which = lax.broadcasted_iota(jnp.int32, (16, row.shape[1]), 0)
    pieces = jnp.where(which == 0, high, jnp.where(which == 1, middle, jnp.where(which == 2, row - high - middle, 0.0)))
    return pieces.astype(bf16)


def slope_kernel(which, core_ref, parts_ref, column_ref, total_ref, target_ref, expo_ref, rows_ref, out_ref, columns):
    groups, both, depth = rows_ref.shape
    count = both // 2
    n, width, _ = out_ref.shape
    width = width - 16
    column = half_columns(core_ref, column_ref, columns)[which]
    sums = total_of(parts_ref)
    lines = sums.shape[0] // 2
    row = 1.0 / sums[:lines]
    student_total = total_ref[...]
    partial = jnp.sum(jnp.log(student_total)) - jnp.sum(row * sums[lines:])
    row = unfold(row * student_scale)
    inverse = unfold(student_scale / student_total)
    column = jnp.broadcast_to(column, (8, n * width)).T[:, 0:1]
    for i in range(n):
        grad = jnp.zeros((width, depth), f32)
        for j in range(groups):
            lanes = slice(count * j, count * (j + 1))
            place = (slice(width * i, width * (i + 1)), lanes)
            target = target_ref[place].astype(f32) * column[width * i : width * (i + 1)] * row[:, lanes]
            slope = (expo_ref[place].astype(f32) * inverse[:, lanes] - target).astype(bf16)
            grad = grad + dot(slope, rows_ref[j, count:], NN)
        out_ref[i, :width] = grad.astype(out_ref.dtype)
        out_ref[i, width:] = pieces_of(jnp.full((1, depth), partial, f32)).astype(out_ref.dtype)


def join_kernel(own_ref, other_ref, out_ref):
    width = own_ref.shape[1] - 16
    for i in range(own_ref.shape[0]):
        out_ref[i, :width] = (own_ref[i, :width] + other_ref[i, :width].astype(f32)).astype(bf16)
        pieces = own_ref[i, width:] + other_ref[i, width:].astype(f32)
        out_ref[i, width:] = pieces_of(jnp.sum(pieces, axis=0, keepdims=True))


def finish_kernel(rows, parts_ref, proto_ref, loss_ref, grad_ref):
    width = proto_ref.shape[0]
    unit_grad = parts_ref[0, :width].astype(f32)
    pieces = parts_ref[0, width:].astype(f32)
    for i in range(1, parts_ref.shape[0]):
        unit_grad = unit_grad + parts_ref[i, :width].astype(f32)
        pieces = pieces + parts_ref[i, width:].astype(f32)
    loss_ref[...] = jnp.sum(pieces, axis=0, keepdims=True)[:, :LANES] / rows
    proto = proto_ref[...].astype(f32)
    scale = lax.rsqrt(jnp.sum(proto * proto, axis=1, keepdims=True) + norm_eps)
    unit = proto * scale
    grad_ref[...] = (unit_grad - unit * jnp.sum(unit * unit_grad, axis=1, keepdims=True)) * scale


def call(kernel, outs, *args, place=None, scratch=(), limit=20):
    vmem = pl.BlockSpec(memory_space=pltpu.VMEM)
    place = place or {}
    return pl.pallas_call(
        kernel,
        out_shape=outs,
        in_specs=[pl.BlockSpec(memory_space=place[i]) if i in place else vmem for i in range(len(args))],
        out_specs=jax.tree.map(lambda _: vmem, outs),
        scratch_shapes=scratch,
        compiler_params=pltpu.CompilerParams(vmem_limit_bytes=limit * 1024 * 1024),
    )(*args)


def per_device(nz, ny, nx, nc, student_patches, teacher_patches, mask_rows, student_proto, teacher_proto):
    shape = jax.ShapeDtypeStruct
    held = pltpu.VMEM
    count = mask_rows.shape[0]
    patches = student_patches.shape
    width, depth = student_proto.shape
    rows = count * nz * ny
    columns = width * nx * nc
    lines, column_lines = rows // LANES, columns // LANES

    def exchange(values, axes):
        return lax.all_to_all(values, axes, 0, 0, tiled=True)

    def far(values):
        return pltpu.with_memory_space_constraint(values, pltpu.HBM)

    def sems(n):
        return pltpu.SemaphoreType.DMA((n,))

    picked = call(
        rows_kernel,
        shape((nz, 2 * count, depth), bf16),
        far(mask_rows), far(student_patches), far(teacher_patches),
        place={0: pltpu.HBM, 1: pltpu.HBM, 2: pltpu.HBM},
        scratch=[pltpu.SMEM((count,), jnp.int32), pltpu.VMEM(patches, bf16), pltpu.VMEM(patches, bf16), sems(3)],
    )
    late_teacher, late_student, picked = lax.optimization_barrier((teacher_proto, student_proto, picked))
    weights = call(
        weights_kernel,
        shape((2, width, depth), bf16),
        far(late_teacher), far(late_student),
        place={0: pltpu.HBM, 1: pltpu.HBM},
        scratch=[pltpu.VMEM((width, depth), bf16), pltpu.VMEM((width, depth), bf16), sems(2)],
    )
    parts = [weights] + [lax.ppermute(weights, "x", [(i, (i + k) % nx) for i in range(nx)]) for k in range(1, nx)]
    core = lax.axis_index("c").astype(jnp.int32).reshape(1)
    places = (lax.axis_index("x") - jnp.arange(nx, dtype=jnp.int32)) % nx
    places, core, picked = lax.optimization_barrier((places, core, picked))
    picked = exchange(picked, "z")
    picked, parts[2] = lax.optimization_barrier((picked, parts[2]))
    picked = call(divide_kernel, shape((ny, 2 * nz * count, depth), bf16), picked)
    picked = exchange(picked, "y")
    picked, *parts = lax.optimization_barrier((picked, *parts))
    own_weights = call(
        place_kernel,
        shape((nx, *weights.shape), bf16),
        places, *parts,
        place={0: pltpu.SMEM, **{1 + i: pl.ANY for i in range(nx)}},
        scratch=[sems(nx)],
    )
    other_weights = lax.ppermute(own_weights, "c", [(i, (i + 1) % nc) for i in range(nc)])

    matrix = held((nx * width, rows), bf16)
    half_out = (matrix, matrix, matrix, shape((lines, LANES), f32), shape((column_lines // nc, LANES), f32))
    own_target, own_expo, own_product, own_total, own_sums = call(half_kernel, half_out, picked, own_weights)
    other_target, other_expo, other_product, other_total, other_sums = call(half_kernel, half_out, picked, other_weights)
    targets = (own_target, other_target)

    smem = {0: pltpu.SMEM}
    scratch = [pltpu.VMEM((column_lines, LANES), f32)]
    column_out = shape((nx * nc, column_lines, LANES), f32)
    row_out = shape((ny, lines, LANES), f32)
    rows_out = shape((ny, 2 * lines, LANES), f32)
    column = call(join_first_kernel, column_out, core, own_sums, other_sums, place=smem)
    column = exchange(column, ("c", "x"))
    row = call(row_kernel, row_out, core, column, *targets, place=smem, scratch=scratch)
    row = exchange(row, "y")
    row = call(add_kernel, shape((nz, lines, LANES), f32), row)
    row = exchange(row, "z")

    column = call(column_kernel, column_out, core, row, *targets, place=smem)
    column = exchange(column, ("c", "x"))
    row = call(second_row_kernel, rows_out, core, column, *targets, own_total, other_total, place=smem, scratch=scratch)
    row = exchange(row, "y")
    row = call(add_kernel, shape((nz, 2 * lines, LANES), f32), row)
    row = exchange(row, "z")

    column, student_total = call(
        third_column_kernel, (column_out, shape((lines, LANES), f32)), core, row, *targets, place=smem
    )
    column = exchange(column, ("c", "x"))
    row = call(
        last_row_kernel, rows_out, core, column, *targets, own_product, other_product, place=smem, scratch=scratch
    )
    row = exchange(row, "y")
    row = call(add_kernel, shape((nz, 2 * lines, LANES), f32), row)
    row = exchange(row, "z")

    halves = []
    for which, kind, target, expo in ((1, bf16, other_target, other_expo), (0, f32, own_target, own_expo)):
        halves.append(
            call(
                functools.partial(slope_kernel, which),
                shape((nx, width + 16, depth), kind),
                core, row, column, student_total, target, expo, picked,
                place=smem,
                scratch=scratch,
            )
        )
    other = lax.ppermute(halves[0], "c", [(i, (i + 1) % nc) for i in range(nc)])
    grads = call(join_kernel, shape((nx, width + 16, depth), bf16), halves[1], other)
    grads = exchange(grads, "x")
    loss, proto_grad = call(
        lambda *refs: finish_kernel(rows * nx * nc, *refs),
        (shape((1, LANES), f32), shape((width, depth), f32)),
        grads, student_proto,
    )
    return (loss[0, 0], proto_grad)


def solution(mesh):
    nz = mesh.shape["grp"]
    ny, nx, nc = 4, 4, 2
    axes = ("z", "y", "x", "c")
    inner = Mesh(mesh.devices.reshape(nz, ny, nx, nc), axes)
    placed = (P(axes, None), P(axes, None), P(axes), P(axes, None), P(axes, None))
    return jax.shard_map(
        lambda *args: per_device(nz, ny, nx, nc, *args),
        mesh=inner,
        in_specs=placed,
        out_specs=(P(), P(axes, None)),
        check_vma=False,
    )
```

```python
import functools

import jax
import jax.numpy as jnp
from jax import lax
from jax.experimental import pallas as pl
from jax.experimental.pallas import tpu as pltpu
from jax.sharding import Mesh, PartitionSpec as P

LANES = 128

norm_eps = 1e-06
teacher_scale = 1.0 / 0.07
student_scale = 1.0 / 0.1
log2_e = 1.4426950408889634

f32 = jnp.float32
bf16 = jnp.bfloat16
NT = (((1,), (1,)), ((), ()))
NN = (((1,), (0,)), ((), ()))


def dot(a, b, dims):
    return lax.dot_general(a, b, dims, preferred_element_type=f32)


def unit_rows(values):
    values = values.astype(f32)
    return values * lax.rsqrt(jnp.sum(values * values, axis=1, keepdims=True) + norm_eps)


def fold(row):
    n = row.shape[1] // LANES
    return jnp.concatenate([row[:, LANES * i : LANES * (i + 1)] for i in range(n)], axis=0)


def unfold(tile):
    return jnp.concatenate([tile[i : i + 1, :] for i in range(tile.shape[0])], axis=1)


def split_rows(row):
    high = row.astype(bf16).astype(f32)
    which = lax.broadcasted_iota(jnp.int32, (16, row.shape[1]), 0)
    return jnp.where(which == 0, high, jnp.where(which == 1, row - high, 0.0)).astype(bf16)


def matvec(row, matrix, dims):
    return jnp.sum(dot(split_rows(row), matrix, dims), axis=0, keepdims=True)


def spread(out_ref, tile):
    tile = tile.astype(out_ref.dtype)
    for i in range(out_ref.shape[0]):
        out_ref[i] = tile


def total_of(parts_ref):
    total = parts_ref[0].astype(f32)
    for i in range(1, parts_ref.shape[0]):
        total = total + parts_ref[i].astype(f32)
    return total


def rows_kernel(mask_ref, sp_ref, tp_ref, rows_ref, mask, sp, tp, sems):
    copies = [
        pltpu.make_async_copy(source, target, sems.at[i])
        for i, (source, target) in enumerate(((mask_ref, mask), (tp_ref, tp), (sp_ref, sp)))
    ]
    for copy in copies:
        copy.start()
    count = mask_ref.shape[0]
    patches = sp_ref.shape[0]
    copies[0].wait()
    which = lax.broadcasted_iota(jnp.int32, (count, patches), 0)
    wanted = jnp.zeros((count, patches), jnp.int32)
    for i in range(count):
        wanted = jnp.where(which == i, mask[i], wanted)
    onehot = (lax.broadcasted_iota(jnp.int32, (count, patches), 1) == wanted).astype(f32).astype(bf16)
    copies[1].wait()
    teacher = unit_rows(dot(onehot, tp[...], NN)).astype(bf16)
    copies[2].wait()
    student = unit_rows(dot(onehot, sp[...], NN)).astype(bf16)
    for i in range(rows_ref.shape[0]):
        rows_ref[i, :count] = teacher
        rows_ref[i, count:] = student


def weights_kernel(tw_ref, sw_ref, weights_ref, tw, sw, sems):
    copies = [
        pltpu.make_async_copy(source, target, sems.at[i])
        for i, (source, target) in enumerate(((tw_ref, tw), (sw_ref, sw)))
    ]
    for copy in copies:
        copy.start()
    copies[0].wait()
    weights_ref[0] = unit_rows(tw[...]).astype(bf16)
    copies[1].wait()
    weights_ref[1] = unit_rows(sw[...]).astype(bf16)


def divide_kernel(rows_ref, out_ref):
    n, both, _ = rows_ref.shape
    count = both // 2
    for i in range(n):
        for j in range(out_ref.shape[0]):
            out_ref[j, count * i : count * (i + 1)] = rows_ref[i, :count]
            out_ref[j, count * (n + i) : count * (n + i + 1)] = rows_ref[i, count:]


def place_kernel(place_ref, *refs):
    *parts, out_ref, sems = refs
    copies = [
        pltpu.make_async_copy(part, out_ref.at[place_ref[i]], sems.at[i]) for i, part in enumerate(parts)
    ]
    for copy in copies:
        copy.start()
    for copy in copies:
        copy.wait()


def half_kernel(rows_ref, weights_ref, target_ref, expo_ref, product_ref, total_ref, sums_ref):
    groups, both, _ = rows_ref.shape
    count = both // 2
    nx, _, width, _ = weights_ref.shape
    for j in range(groups):
        total = jnp.zeros((1, count), f32)
        for i in range(nx):
            place = (slice(width * i, width * (i + 1)), slice(count * j, count * (j + 1)))
            target = jnp.exp2(dot(weights_ref[i, 0], rows_ref[j, :count], NT) * (teacher_scale * log2_e))
            score = dot(weights_ref[i, 1], rows_ref[j, count:], NT)
            expo = jnp.exp2(score * (student_scale * log2_e))
            total = total + jnp.sum(expo, axis=0, keepdims=True)
            target_ref[place] = target.astype(bf16)
            expo_ref[place] = expo.astype(bf16)
            product_ref[place] = (target * score).astype(bf16)
        per = count // LANES
        total_ref[per * j : per * (j + 1)] = fold(total)
    sums_ref[...] = fold(matvec(jnp.ones((1, groups * count), f32), target_ref[...], NT))


def spread_halves(core_ref, out_ref, own, other):
    first = core_ref[0] == 0
    spread(out_ref, jnp.concatenate([jnp.where(first, own, other), jnp.where(first, other, own)], axis=0))


def half_columns(core_ref, parts_ref, columns):
    columns[...] = 1.0 / total_of(parts_ref)
    core = core_ref[0]
    lines = columns.shape[0] // 2
    own = columns[pl.ds(pl.multiple_of(core * lines, lines), lines), :]
    other = columns[pl.ds(pl.multiple_of((1 - core) * lines, lines), lines), :]
    return unfold(own), unfold(other)


def join_first_kernel(core_ref, own_ref, other_ref, column_ref):
    spread_halves(core_ref, column_ref, own_ref[...], other_ref[...])


def column_kernel(core_ref, parts_ref, own_ref, other_ref, column_ref):
    row = unfold(1.0 / total_of(parts_ref))
    spread_halves(core_ref, column_ref, fold(matvec(row, own_ref[...], NT)), fold(matvec(row, other_ref[...], NT)))


def third_column_kernel(core_ref, parts_ref, own_ref, other_ref, column_ref, total_ref):
    both = total_of(parts_ref)
    lines = both.shape[0] // 2
    row = unfold(1.0 / both[:lines])
    spread_halves(core_ref, column_ref, fold(matvec(row, own_ref[...], NT)), fold(matvec(row, other_ref[...], NT)))
    total_ref[...] = both[lines:]


def row_kernel(core_ref, parts_ref, own_ref, other_ref, out_ref, columns):
    own, other = half_columns(core_ref, parts_ref, columns)
    spread(out_ref, fold(matvec(own, own_ref[...], NN) + matvec(other, other_ref[...], NN)))


def second_row_kernel(core_ref, parts_ref, own_ref, other_ref, own_total_ref, other_total_ref, out_ref, columns):
    own, other = half_columns(core_ref, parts_ref, columns)
    sums = fold(matvec(own, own_ref[...], NN) + matvec(other, other_ref[...], NN))
    spread(out_ref, jnp.concatenate([sums, own_total_ref[...] + other_total_ref[...]], axis=0))


def last_row_kernel(core_ref, parts_ref, own_ref, other_ref, own_product_ref, other_product_ref, out_ref, columns):
    own, other = half_columns(core_ref, parts_ref, columns)
    sums = fold(matvec(own, own_ref[...], NN) + matvec(other, other_ref[...], NN))
    cross = fold(matvec(own, own_product_ref[...], NN) + matvec(other, other_product_ref[...], NN)) * student_scale
    spread(out_ref, jnp.concatenate([sums, cross], axis=0))


def add_kernel(parts_ref, out_ref):
    spread(out_ref, total_of(parts_ref))


def pieces_of(row):
    high = row.astype(bf16).astype(f32)
    middle = (row - high).astype(bf16).astype(f32)
    which = lax.broadcasted_iota(jnp.int32, (16, row.shape[1]), 0)
    pieces = jnp.where(which == 0, high, jnp.where(which == 1, middle, jnp.where(which == 2, row - high - middle, 0.0)))
    return pieces.astype(bf16)


def slope_kernel(which, core_ref, parts_ref, column_ref, total_ref, target_ref, expo_ref, rows_ref, out_ref, columns):
    groups, both, depth = rows_ref.shape
    count = both // 2
    n, width, _ = out_ref.shape
    width = width - 16
    column = half_columns(core_ref, column_ref, columns)[which]
    sums = total_of(parts_ref)
    lines = sums.shape[0] // 2
    row = 1.0 / sums[:lines]
    student_total = total_ref[...]
    partial = jnp.sum(jnp.log(student_total)) - jnp.sum(row * sums[lines:])
    row = unfold(row * student_scale)
    inverse = unfold(student_scale / student_total)
    column = jnp.broadcast_to(column, (8, n * width)).T[:, 0:1]
    for i in range(n):
        grad = jnp.zeros((width, depth), f32)
        for j in range(groups):
            lanes = slice(count * j, count * (j + 1))
            place = (slice(width * i, width * (i + 1)), lanes)
            target = target_ref[place].astype(f32) * column[width * i : width * (i + 1)] * row[:, lanes]
            slope = (expo_ref[place].astype(f32) * inverse[:, lanes] - target).astype(bf16)
            grad = grad + dot(slope, rows_ref[j, count:], NN)
        out_ref[i, :width] = grad.astype(out_ref.dtype)
        out_ref[i, width:] = pieces_of(jnp.full((1, depth), partial, f32)).astype(out_ref.dtype)


def join_kernel(own_ref, other_ref, out_ref):
    width = own_ref.shape[1] - 16
    for i in range(own_ref.shape[0]):
        out_ref[i, :width] = (own_ref[i, :width] + other_ref[i, :width].astype(f32)).astype(bf16)
        pieces = own_ref[i, width:] + other_ref[i, width:].astype(f32)
        out_ref[i, width:] = pieces_of(jnp.sum(pieces, axis=0, keepdims=True))


def finish_kernel(rows, parts_ref, proto_ref, loss_ref, grad_ref):
    width = proto_ref.shape[0]
    unit_grad = parts_ref[0, :width].astype(f32)
    pieces = parts_ref[0, width:].astype(f32)
    for i in range(1, parts_ref.shape[0]):
        unit_grad = unit_grad + parts_ref[i, :width].astype(f32)
        pieces = pieces + parts_ref[i, width:].astype(f32)
    loss_ref[...] = jnp.sum(pieces, axis=0, keepdims=True)[:, :LANES] / rows
    proto = proto_ref[...].astype(f32)
    scale = lax.rsqrt(jnp.sum(proto * proto, axis=1, keepdims=True) + norm_eps)
    unit = proto * scale
    grad_ref[...] = (unit_grad - unit * jnp.sum(unit * unit_grad, axis=1, keepdims=True)) * scale


def call(kernel, outs, *args, place=None, scratch=(), limit=20):
    vmem = pl.BlockSpec(memory_space=pltpu.VMEM)
    place = place or {}
    return pl.pallas_call(
        kernel,
        out_shape=outs,
        in_specs=[pl.BlockSpec(memory_space=place[i]) if i in place else vmem for i in range(len(args))],
        out_specs=jax.tree.map(lambda _: vmem, outs),
        scratch_shapes=scratch,
        compiler_params=pltpu.CompilerParams(vmem_limit_bytes=limit * 1024 * 1024),
    )(*args)


def per_device(nz, ny, nx, nc, student_patches, teacher_patches, mask_rows, student_proto, teacher_proto):
    shape = jax.ShapeDtypeStruct
    held = pltpu.VMEM
    count = mask_rows.shape[0]
    patches = student_patches.shape
    width, depth = student_proto.shape
    rows = count * nz * ny
    columns = width * nx * nc
    lines, column_lines = rows // LANES, columns // LANES

    def exchange(values, axes):
        return lax.all_to_all(values, axes, 0, 0, tiled=True)

    def far(values):
        return pltpu.with_memory_space_constraint(values, pltpu.HBM)

    def sems(n):
        return pltpu.SemaphoreType.DMA((n,))

    picked = call(
        rows_kernel,
        shape((nz, 2 * count, depth), bf16),
        far(mask_rows), far(student_patches), far(teacher_patches),
        place={0: pltpu.HBM, 1: pltpu.HBM, 2: pltpu.HBM},
        scratch=[pltpu.SMEM((count,), jnp.int32), pltpu.VMEM(patches, bf16), pltpu.VMEM(patches, bf16), sems(3)],
    )
    late_teacher, late_student, picked = lax.optimization_barrier((teacher_proto, student_proto, picked))
    weights = call(
        weights_kernel,
        shape((2, width, depth), bf16),
        far(late_teacher), far(late_student),
        place={0: pltpu.HBM, 1: pltpu.HBM},
        scratch=[pltpu.VMEM((width, depth), bf16), pltpu.VMEM((width, depth), bf16), sems(2)],
    )
    parts = [weights] + [lax.ppermute(weights, "x", [(i, (i + k) % nx) for i in range(nx)]) for k in range(1, nx)]
    core = lax.axis_index("c").astype(jnp.int32).reshape(1)
    places = (lax.axis_index("x") - jnp.arange(nx, dtype=jnp.int32)) % nx
    places, core, picked = lax.optimization_barrier((places, core, picked))
    picked = exchange(picked, "z")
    picked, parts[2] = lax.optimization_barrier((picked, parts[2]))
    picked = call(divide_kernel, shape((ny, 2 * nz * count, depth), bf16), picked)
    picked = exchange(picked, "y")
    picked, *parts = lax.optimization_barrier((picked, *parts))
    own_weights = call(
        place_kernel,
        shape((nx, *weights.shape), bf16),
        places, *parts,
        place={0: pltpu.SMEM, **{1 + i: pl.ANY for i in range(nx)}},
        scratch=[sems(nx)],
    )
    other_weights = lax.ppermute(own_weights, "c", [(i, (i + 1) % nc) for i in range(nc)])

    matrix = held((nx * width, rows), bf16)
    half_out = (matrix, matrix, matrix, shape((lines, LANES), f32), shape((column_lines // nc, LANES), f32))
    own_target, own_expo, own_product, own_total, own_sums = call(half_kernel, half_out, picked, own_weights)
    other_target, other_expo, other_product, other_total, other_sums = call(half_kernel, half_out, picked, other_weights)
    targets = (own_target, other_target)

    smem = {0: pltpu.SMEM}
    scratch = [pltpu.VMEM((column_lines, LANES), f32)]
    column_out = shape((nx * nc, column_lines, LANES), bf16)
    row_out = shape((ny, lines, LANES), f32)
    rows_out = shape((ny, 2 * lines, LANES), f32)
    column = call(join_first_kernel, column_out, core, own_sums, other_sums, place=smem)
    column = exchange(column, ("c", "x"))
    row = call(row_kernel, row_out, core, column, *targets, place=smem, scratch=scratch)
    row = exchange(row, "y")
    row = call(add_kernel, shape((nz, lines, LANES), f32), row)
    row = exchange(row, "z")

    column = call(column_kernel, column_out, core, row, *targets, place=smem)
    column = exchange(column, ("c", "x"))
    row = call(second_row_kernel, rows_out, core, column, *targets, own_total, other_total, place=smem, scratch=scratch)
    row = exchange(row, "y")
    row = call(add_kernel, shape((nz, 2 * lines, LANES), bf16), row)
    row = exchange(row, "z")

    column, student_total = call(
        third_column_kernel, (column_out, shape((lines, LANES), f32)), core, row, *targets, place=smem
    )
    column = exchange(column, ("c", "x"))
    row = call(
        last_row_kernel, rows_out, core, column, *targets, own_product, other_product, place=smem, scratch=scratch
    )
    row = exchange(row, "y")
    row = call(add_kernel, shape((nz, 2 * lines, LANES), bf16), row)
    row = exchange(row, "z")

    halves = []
    for which, kind, target, expo in ((1, bf16, other_target, other_expo), (0, f32, own_target, own_expo)):
        halves.append(
            call(
                functools.partial(slope_kernel, which),
                shape((nx, width + 16, depth), kind),
                core, row, column, student_total, target, expo, picked,
                place=smem,
                scratch=scratch,
            )
        )
    other = lax.ppermute(halves[0], "c", [(i, (i + 1) % nc) for i in range(nc)])
    grads = call(join_kernel, shape((nx, width + 16, depth), bf16), halves[1], other)
    grads = exchange(grads, "x")
    loss, proto_grad = call(
        lambda *refs: finish_kernel(rows * nx * nc, *refs),
        (shape((1, LANES), f32), shape((width, depth), f32)),
        grads, student_proto,
    )
    return (loss[0, 0], proto_grad)


def solution(mesh):
    nz = mesh.shape["grp"]
    ny, nx, nc = 4, 4, 2
    axes = ("z", "y", "x", "c")
    inner = Mesh(mesh.devices.reshape(nz, ny, nx, nc), axes)
    placed = (P(axes, None), P(axes, None), P(axes), P(axes, None), P(axes, None))
    return jax.shard_map(
        lambda *args: per_device(nz, ny, nx, nc, *args),
        mesh=inner,
        in_specs=placed,
        out_specs=(P(), P(axes, None)),
        check_vma=False,
    )
```

```python
import functools

import jax
import jax.numpy as jnp
from jax import lax
from jax.experimental import pallas as pl
from jax.experimental.pallas import tpu as pltpu
from jax.sharding import Mesh, PartitionSpec as P

LANES = 128

norm_eps = 1e-06
teacher_scale = 1.0 / 0.07
student_scale = 1.0 / 0.1
log2_e = 1.4426950408889634

f32 = jnp.float32
bf16 = jnp.bfloat16
NT = (((1,), (1,)), ((), ()))
NN = (((1,), (0,)), ((), ()))


def dot(a, b, dims):
    return lax.dot_general(a, b, dims, preferred_element_type=f32)


def unit_rows(values):
    values = values.astype(f32)
    return values * lax.rsqrt(jnp.sum(values * values, axis=1, keepdims=True) + norm_eps)


def fold(row):
    n = row.shape[1] // LANES
    return jnp.concatenate([row[:, LANES * i : LANES * (i + 1)] for i in range(n)], axis=0)


def unfold(tile):
    return jnp.concatenate([tile[i : i + 1, :] for i in range(tile.shape[0])], axis=1)


def split_rows(row):
    high = row.astype(bf16).astype(f32)
    which = lax.broadcasted_iota(jnp.int32, (16, row.shape[1]), 0)
    return jnp.where(which == 0, high, jnp.where(which == 1, row - high, 0.0)).astype(bf16)


def matvec(row, matrix, dims):
    return jnp.sum(dot(split_rows(row), matrix, dims), axis=0, keepdims=True)


def spread(out_ref, tile):
    tile = tile.astype(out_ref.dtype)
    for i in range(out_ref.shape[0]):
        out_ref[i] = tile


def total_of(parts_ref):
    total = parts_ref[0].astype(f32)
    for i in range(1, parts_ref.shape[0]):
        total = total + parts_ref[i].astype(f32)
    return total


def rows_kernel(mask_ref, sp_ref, tp_ref, rows_ref, mask, sp, tp, sems):
    copies = [
        pltpu.make_async_copy(source, target, sems.at[i])
        for i, (source, target) in enumerate(((mask_ref, mask), (tp_ref, tp), (sp_ref, sp)))
    ]
    for copy in copies:
        copy.start()
    count = mask_ref.shape[0]
    patches = sp_ref.shape[0]
    copies[0].wait()
    which = lax.broadcasted_iota(jnp.int32, (count, patches), 0)
    wanted = jnp.zeros((count, patches), jnp.int32)
    for i in range(count):
        wanted = jnp.where(which == i, mask[i], wanted)
    onehot = (lax.broadcasted_iota(jnp.int32, (count, patches), 1) == wanted).astype(f32).astype(bf16)
    copies[1].wait()
    teacher = unit_rows(dot(onehot, tp[...], NN)).astype(bf16)
    copies[2].wait()
    student = unit_rows(dot(onehot, sp[...], NN)).astype(bf16)
    for i in range(rows_ref.shape[0]):
        rows_ref[i, :count] = teacher
        rows_ref[i, count:] = student


def weights_kernel(tw_ref, sw_ref, weights_ref, tw, sw, sems):
    copies = [
        pltpu.make_async_copy(source, target, sems.at[i])
        for i, (source, target) in enumerate(((tw_ref, tw), (sw_ref, sw)))
    ]
    for copy in copies:
        copy.start()
    copies[0].wait()
    weights_ref[0] = unit_rows(tw[...]).astype(bf16)
    copies[1].wait()
    weights_ref[1] = unit_rows(sw[...]).astype(bf16)


def divide_kernel(rows_ref, out_ref):
    n, both, _ = rows_ref.shape
    count = both // 2
    for i in range(n):
        for j in range(out_ref.shape[0]):
            out_ref[j, count * i : count * (i + 1)] = rows_ref[i, :count]
            out_ref[j, count * (n + i) : count * (n + i + 1)] = rows_ref[i, count:]


def place_kernel(place_ref, *refs):
    *parts, out_ref, sems = refs
    copies = [
        pltpu.make_async_copy(part, out_ref.at[place_ref[i]], sems.at[i]) for i, part in enumerate(parts)
    ]
    for copy in copies:
        copy.start()
    for copy in copies:
        copy.wait()


def half_kernel(rows_ref, weights_ref, target_ref, expo_ref, product_ref, total_ref, sums_ref):
    groups, both, _ = rows_ref.shape
    count = both // 2
    nx, _, width, _ = weights_ref.shape
    for j in range(groups):
        total = jnp.zeros((1, count), f32)
        for i in range(nx):
            place = (slice(width * i, width * (i + 1)), slice(count * j, count * (j + 1)))
            target = jnp.exp2(dot(weights_ref[i, 0], rows_ref[j, :count], NT) * (teacher_scale * log2_e))
            score = dot(weights_ref[i, 1], rows_ref[j, count:], NT)
            expo = jnp.exp2(score * (student_scale * log2_e))
            total = total + jnp.sum(expo, axis=0, keepdims=True)
            target_ref[place] = target.astype(bf16)
            expo_ref[place] = expo.astype(bf16)
            product_ref[place] = (target * score).astype(bf16)
        per = count // LANES
        total_ref[per * j : per * (j + 1)] = fold(total)
    sums_ref[...] = fold(matvec(jnp.ones((1, groups * count), f32), target_ref[...], NT))


def spread_halves(core_ref, out_ref, own, other):
    first = core_ref[0] == 0
    spread(out_ref, jnp.concatenate([jnp.where(first, own, other), jnp.where(first, other, own)], axis=0))


def half_columns(core_ref, parts_ref, columns):
    columns[...] = 1.0 / total_of(parts_ref)
    core = core_ref[0]
    lines = columns.shape[0] // 2
    own = columns[pl.ds(pl.multiple_of(core * lines, lines), lines), :]
    other = columns[pl.ds(pl.multiple_of((1 - core) * lines, lines), lines), :]
    return unfold(own), unfold(other)


def join_first_kernel(core_ref, own_ref, other_ref, column_ref):
    spread_halves(core_ref, column_ref, own_ref[...], other_ref[...])


def column_kernel(core_ref, parts_ref, own_ref, other_ref, column_ref):
    row = unfold(1.0 / total_of(parts_ref))
    spread_halves(core_ref, column_ref, fold(matvec(row, own_ref[...], NT)), fold(matvec(row, other_ref[...], NT)))


def third_column_kernel(core_ref, parts_ref, own_ref, other_ref, column_ref, total_ref):
    both = total_of(parts_ref)
    lines = both.shape[0] // 2
    row = unfold(1.0 / both[:lines])
    spread_halves(core_ref, column_ref, fold(matvec(row, own_ref[...], NT)), fold(matvec(row, other_ref[...], NT)))
    total_ref[...] = both[lines:]


def row_kernel(core_ref, parts_ref, own_ref, other_ref, out_ref, columns):
    own, other = half_columns(core_ref, parts_ref, columns)
    spread(out_ref, fold(matvec(own, own_ref[...], NN) + matvec(other, other_ref[...], NN)))


def second_row_kernel(core_ref, parts_ref, own_ref, other_ref, own_total_ref, other_total_ref, out_ref, columns):
    own, other = half_columns(core_ref, parts_ref, columns)
    sums = fold(matvec(own, own_ref[...], NN) + matvec(other, other_ref[...], NN))
    spread(out_ref, jnp.concatenate([sums, own_total_ref[...] + other_total_ref[...]], axis=0))


def last_row_kernel(core_ref, parts_ref, own_ref, other_ref, own_product_ref, other_product_ref, out_ref, columns):
    own, other = half_columns(core_ref, parts_ref, columns)
    sums = fold(matvec(own, own_ref[...], NN) + matvec(other, other_ref[...], NN))
    cross = fold(matvec(own, own_product_ref[...], NN) + matvec(other, other_product_ref[...], NN)) * student_scale
    spread(out_ref, jnp.concatenate([sums, cross], axis=0))


def add_kernel(parts_ref, out_ref):
    spread(out_ref, total_of(parts_ref))


def pieces_of(row):
    high = row.astype(bf16).astype(f32)
    middle = (row - high).astype(bf16).astype(f32)
    which = lax.broadcasted_iota(jnp.int32, (16, row.shape[1]), 0)
    pieces = jnp.where(which == 0, high, jnp.where(which == 1, middle, jnp.where(which == 2, row - high - middle, 0.0)))
    return pieces.astype(bf16)


def slope_kernel(which, core_ref, parts_ref, column_ref, total_ref, target_ref, expo_ref, rows_ref, out_ref, columns):
    groups, both, depth = rows_ref.shape
    count = both // 2
    n, width, _ = out_ref.shape
    width = width - 16
    column = half_columns(core_ref, column_ref, columns)[which]
    sums = total_of(parts_ref)
    lines = sums.shape[0] // 2
    row = 1.0 / sums[:lines]
    student_total = total_ref[...]
    partial = jnp.sum(jnp.log(student_total)) - jnp.sum(row * sums[lines:])
    row = unfold(row * student_scale)
    inverse = unfold(student_scale / student_total)
    column = jnp.broadcast_to(column, (8, n * width)).T[:, 0:1]
    for i in range(n):
        grad = jnp.zeros((width, depth), f32)
        for j in range(groups):
            lanes = slice(count * j, count * (j + 1))
            place = (slice(width * i, width * (i + 1)), lanes)
            target = target_ref[place].astype(f32) * column[width * i : width * (i + 1)] * row[:, lanes]
            slope = (expo_ref[place].astype(f32) * inverse[:, lanes] - target).astype(bf16)
            grad = grad + dot(slope, rows_ref[j, count:], NN)
        out_ref[i, :width] = grad.astype(out_ref.dtype)
        out_ref[i, width:] = pieces_of(jnp.full((1, depth), partial, f32)).astype(out_ref.dtype)


def join_kernel(own_ref, other_ref, out_ref):
    n, width, _ = own_ref.shape
    width = width - 16
    for j, i in enumerate(half_turn(n)):
        out_ref[j, :width] = (own_ref[i, :width] + other_ref[i, :width].astype(f32)).astype(bf16)
        pieces = own_ref[i, width:] + other_ref[i, width:].astype(f32)
        out_ref[j, width:] = pieces_of(jnp.sum(pieces, axis=0, keepdims=True))


def finish_kernel(rows, parts_ref, proto_ref, loss_ref, grad_ref):
    width = proto_ref.shape[0]
    unit_grad = parts_ref[0, :width].astype(f32)
    pieces = parts_ref[0, width:].astype(f32)
    for i in range(1, parts_ref.shape[0]):
        unit_grad = unit_grad + parts_ref[i, :width].astype(f32)
        pieces = pieces + parts_ref[i, width:].astype(f32)
    loss_ref[...] = jnp.sum(pieces, axis=0, keepdims=True)[:, :LANES] / rows
    proto = proto_ref[...].astype(f32)
    scale = lax.rsqrt(jnp.sum(proto * proto, axis=1, keepdims=True) + norm_eps)
    unit = proto * scale
    grad_ref[...] = (unit_grad - unit * jnp.sum(unit * unit_grad, axis=1, keepdims=True)) * scale


def half_turn(n):
    return [(i + n // 2) % n for i in range(n)]


def call(kernel, outs, *args, place=None, scratch=(), limit=20):
    vmem = pl.BlockSpec(memory_space=pltpu.VMEM)
    place = place or {}
    return pl.pallas_call(
        kernel,
        out_shape=outs,
        in_specs=[pl.BlockSpec(memory_space=place[i]) if i in place else vmem for i in range(len(args))],
        out_specs=jax.tree.map(lambda _: vmem, outs),
        scratch_shapes=scratch,
        compiler_params=pltpu.CompilerParams(vmem_limit_bytes=limit * 1024 * 1024),
    )(*args)


def per_device(nz, ny, nx, nc, student_patches, teacher_patches, mask_rows, student_proto, teacher_proto):
    shape = jax.ShapeDtypeStruct
    held = pltpu.VMEM
    count = mask_rows.shape[0]
    patches = student_patches.shape
    width, depth = student_proto.shape
    rows = count * nz * ny
    columns = width * nx * nc
    lines, column_lines = rows // LANES, columns // LANES

    orders = {
        "z": half_turn(nz),
        "y": half_turn(ny),
        "x": half_turn(nx),
        ("c", "x"): [c * nx + x for c in reversed(range(nc)) for x in half_turn(nx)],
    }

    def exchange(values, axes):
        return lax.all_to_all(values, axes, 0, 0, axis_index_groups=[orders[axes]], tiled=True)

    def far(values):
        return pltpu.with_memory_space_constraint(values, pltpu.HBM)

    def sems(n):
        return pltpu.SemaphoreType.DMA((n,))

    picked = call(
        rows_kernel,
        shape((nz, 2 * count, depth), bf16),
        far(mask_rows), far(student_patches), far(teacher_patches),
        place={0: pltpu.HBM, 1: pltpu.HBM, 2: pltpu.HBM},
        scratch=[pltpu.SMEM((count,), jnp.int32), pltpu.VMEM(patches, bf16), pltpu.VMEM(patches, bf16), sems(3)],
    )
    late_teacher, late_student, picked = lax.optimization_barrier((teacher_proto, student_proto, picked))
    weights = call(
        weights_kernel,
        shape((2, width, depth), bf16),
        far(late_teacher), far(late_student),
        place={0: pltpu.HBM, 1: pltpu.HBM},
        scratch=[pltpu.VMEM((width, depth), bf16), pltpu.VMEM((width, depth), bf16), sems(2)],
    )
    parts = [weights] + [lax.ppermute(weights, "x", [(i, (i + k) % nx) for i in range(nx)]) for k in range(1, nx)]
    core = lax.axis_index("c").astype(jnp.int32).reshape(1)
    places = (lax.axis_index("x") - jnp.arange(nx, dtype=jnp.int32)) % nx
    places, core, picked = lax.optimization_barrier((places, core, picked))
    picked = exchange(picked, "z")
    picked, parts[2] = lax.optimization_barrier((picked, parts[2]))
    picked = call(divide_kernel, shape((ny, 2 * nz * count, depth), bf16), picked)
    picked = exchange(picked, "y")
    picked, *parts = lax.optimization_barrier((picked, *parts))
    own_weights = call(
        place_kernel,
        shape((nx, *weights.shape), bf16),
        places, *parts,
        place={0: pltpu.SMEM, **{1 + i: pl.ANY for i in range(nx)}},
        scratch=[sems(nx)],
    )
    other_weights = lax.ppermute(own_weights, "c", [(i, (i + 1) % nc) for i in range(nc)])

    matrix = held((nx * width, rows), bf16)
    half_out = (matrix, matrix, matrix, shape((lines, LANES), f32), shape((column_lines // nc, LANES), f32))
    own_target, own_expo, own_product, own_total, own_sums = call(half_kernel, half_out, picked, own_weights)
    other_target, other_expo, other_product, other_total, other_sums = call(half_kernel, half_out, picked, other_weights)
    targets = (own_target, other_target)

    smem = {0: pltpu.SMEM}
    scratch = [pltpu.VMEM((column_lines, LANES), f32)]
    column_out = shape((nx * nc, column_lines, LANES), bf16)
    row_out = shape((ny, lines, LANES), f32)
    rows_out = shape((ny, 2 * lines, LANES), f32)
    column = call(join_first_kernel, column_out, core, own_sums, other_sums, place=smem)
    column = exchange(column, ("c", "x"))
    row = call(row_kernel, row_out, core, column, *targets, place=smem, scratch=scratch)
    row = exchange(row, "y")
    row = call(add_kernel, shape((nz, lines, LANES), f32), row)
    row = exchange(row, "z")

    column = call(column_kernel, column_out, core, row, *targets, place=smem)
    column = exchange(column, ("c", "x"))
    row = call(second_row_kernel, rows_out, core, column, *targets, own_total, other_total, place=smem, scratch=scratch)
    row = exchange(row, "y")
    row = call(add_kernel, shape((nz, 2 * lines, LANES), bf16), row)
    row = exchange(row, "z")

    column, student_total = call(
        third_column_kernel, (column_out, shape((lines, LANES), f32)), core, row, *targets, place=smem
    )
    column = exchange(column, ("c", "x"))
    row = call(
        last_row_kernel, rows_out, core, column, *targets, own_product, other_product, place=smem, scratch=scratch
    )
    row = exchange(row, "y")
    row = call(add_kernel, shape((nz, 2 * lines, LANES), bf16), row)
    row = exchange(row, "z")

    halves = []
    for which, kind, target, expo in ((1, bf16, other_target, other_expo), (0, f32, own_target, own_expo)):
        halves.append(
            call(
                functools.partial(slope_kernel, which),
                shape((nx, width + 16, depth), kind),
                core, row, column, student_total, target, expo, picked,
                place=smem,
                scratch=scratch,
            )
        )
    other = lax.ppermute(halves[0], "c", [(i, (i + 1) % nc) for i in range(nc)])
    grads = call(join_kernel, shape((nx, width + 16, depth), bf16), halves[1], other)
    grads = exchange(grads, "x")
    loss, proto_grad = call(
        lambda *refs: finish_kernel(rows * nx * nc, *refs),
        (shape((1, LANES), f32), shape((width, depth), f32)),
        grads, student_proto,
    )
    return (loss[0, 0], proto_grad)


def solution(mesh):
    nz = mesh.shape["grp"]
    ny, nx, nc = 4, 4, 2
    axes = ("z", "y", "x", "c")
    inner = Mesh(mesh.devices.reshape(nz, ny, nx, nc), axes)
    placed = (P(axes, None), P(axes, None), P(axes), P(axes, None), P(axes, None))
    return jax.shard_map(
        lambda *args: per_device(nz, ny, nx, nc, *args),
        mesh=inner,
        in_specs=placed,
        out_specs=(P(), P(axes, None)),
        check_vma=False,
    )
```

```python
import functools

import jax
import jax.numpy as jnp
from jax import lax
from jax.experimental import pallas as pl
from jax.experimental.pallas import tpu as pltpu
from jax.sharding import Mesh, PartitionSpec as P

LANES = 128

norm_eps = 1e-06
teacher_scale = 1.0 / 0.07
student_scale = 1.0 / 0.1
log2_e = 1.4426950408889634

f32 = jnp.float32
bf16 = jnp.bfloat16
NT = (((1,), (1,)), ((), ()))
NN = (((1,), (0,)), ((), ()))


def dot(a, b, dims):
    return lax.dot_general(a, b, dims, preferred_element_type=f32)


def unit_rows(values):
    values = values.astype(f32)
    return values * lax.rsqrt(jnp.sum(values * values, axis=1, keepdims=True) + norm_eps)


def fold(row):
    n = row.shape[1] // LANES
    return jnp.concatenate([row[:, LANES * i : LANES * (i + 1)] for i in range(n)], axis=0)


def unfold(tile):
    return jnp.concatenate([tile[i : i + 1, :] for i in range(tile.shape[0])], axis=1)


def split_rows(row):
    high = row.astype(bf16).astype(f32)
    which = lax.broadcasted_iota(jnp.int32, (16, row.shape[1]), 0)
    return jnp.where(which == 0, high, jnp.where(which == 1, row - high, 0.0)).astype(bf16)


def matvec(row, matrix, dims):
    return jnp.sum(dot(split_rows(row), matrix, dims), axis=0, keepdims=True)


def spread(out_ref, tile):
    tile = tile.astype(out_ref.dtype)
    for i in range(out_ref.shape[0]):
        out_ref[i] = tile


def total_of(parts_ref):
    total = parts_ref[0].astype(f32)
    for i in range(1, parts_ref.shape[0]):
        total = total + parts_ref[i].astype(f32)
    return total


def rows_kernel(mask_ref, sp_ref, tp_ref, rows_ref, mask, sp, tp, sems):
    copies = [
        pltpu.make_async_copy(source, target, sems.at[i])
        for i, (source, target) in enumerate(((mask_ref, mask), (tp_ref, tp), (sp_ref, sp)))
    ]
    for copy in copies:
        copy.start()
    count = mask_ref.shape[0]
    patches = sp_ref.shape[0]
    copies[0].wait()
    which = lax.broadcasted_iota(jnp.int32, (count, patches), 0)
    wanted = jnp.zeros((count, patches), jnp.int32)
    for i in range(count):
        wanted = jnp.where(which == i, mask[i], wanted)
    onehot = (lax.broadcasted_iota(jnp.int32, (count, patches), 1) == wanted).astype(f32).astype(bf16)
    copies[1].wait()
    teacher = unit_rows(dot(onehot, tp[...], NN)).astype(bf16)
    copies[2].wait()
    student = unit_rows(dot(onehot, sp[...], NN)).astype(bf16)
    for i in range(rows_ref.shape[0]):
        rows_ref[i, :count] = teacher
        rows_ref[i, count:] = student


def weights_kernel(tw_ref, sw_ref, weights_ref, tw, sw, sems):
    copies = [
        pltpu.make_async_copy(source, target, sems.at[i])
        for i, (source, target) in enumerate(((tw_ref, tw), (sw_ref, sw)))
    ]
    for copy in copies:
        copy.start()
    copies[0].wait()
    weights_ref[0] = unit_rows(tw[...]).astype(bf16)
    copies[1].wait()
    weights_ref[1] = unit_rows(sw[...]).astype(bf16)


def divide_kernel(rows_ref, out_ref):
    n, both, _ = rows_ref.shape
    count = both // 2
    for i in range(n):
        for j in range(out_ref.shape[0]):
            out_ref[j, count * i : count * (i + 1)] = rows_ref[i, :count]
            out_ref[j, count * (n + i) : count * (n + i + 1)] = rows_ref[i, count:]


def place_kernel(place_ref, *refs):
    *parts, out_ref, sems = refs
    copies = [
        pltpu.make_async_copy(part, out_ref.at[place_ref[i]], sems.at[i]) for i, part in enumerate(parts)
    ]
    for copy in copies:
        copy.start()
    for copy in copies:
        copy.wait()


def half_kernel(rows_ref, weights_ref, target_ref, expo_ref, product_ref, total_ref, sums_ref):
    groups, both, _ = rows_ref.shape
    count = both // 2
    nx, _, width, _ = weights_ref.shape
    for j in range(groups):
        total = jnp.zeros((1, count), f32)
        for i in range(nx):
            place = (slice(width * i, width * (i + 1)), slice(count * j, count * (j + 1)))
            target = jnp.exp2(dot(weights_ref[i, 0], rows_ref[j, :count], NT) * (teacher_scale * log2_e))
            score = dot(weights_ref[i, 1], rows_ref[j, count:], NT)
            expo = jnp.exp2(score * (student_scale * log2_e))
            total = total + jnp.sum(expo, axis=0, keepdims=True)
            target_ref[place] = target.astype(bf16)
            expo_ref[place] = expo.astype(bf16)
            product_ref[place] = (target * score).astype(bf16)
        per = count // LANES
        total_ref[per * j : per * (j + 1)] = fold(total)
    sums_ref[...] = fold(matvec(jnp.ones((1, groups * count), f32), target_ref[...], NT))


def spread_halves(core_ref, out_ref, own, other):
    first = core_ref[0] == 0
    spread(out_ref, jnp.concatenate([jnp.where(first, own, other), jnp.where(first, other, own)], axis=0))


def half_columns(core_ref, parts_ref, columns):
    columns[...] = 1.0 / total_of(parts_ref)
    core = core_ref[0]
    lines = columns.shape[0] // 2
    own = columns[pl.ds(pl.multiple_of(core * lines, lines), lines), :]
    other = columns[pl.ds(pl.multiple_of((1 - core) * lines, lines), lines), :]
    return unfold(own), unfold(other)


def join_first_kernel(core_ref, own_ref, other_ref, column_ref):
    spread_halves(core_ref, column_ref, own_ref[...], other_ref[...])


def column_kernel(core_ref, parts_ref, own_ref, other_ref, column_ref):
    row = unfold(1.0 / total_of(parts_ref))
    spread_halves(core_ref, column_ref, fold(matvec(row, own_ref[...], NT)), fold(matvec(row, other_ref[...], NT)))


def third_column_kernel(core_ref, parts_ref, own_ref, other_ref, column_ref, total_ref):
    both = total_of(parts_ref)
    lines = both.shape[0] // 2
    row = unfold(1.0 / both[:lines])
    spread_halves(core_ref, column_ref, fold(matvec(row, own_ref[...], NT)), fold(matvec(row, other_ref[...], NT)))
    total_ref[...] = both[lines:]


def row_kernel(core_ref, parts_ref, own_ref, other_ref, out_ref, columns):
    own, other = half_columns(core_ref, parts_ref, columns)
    spread(out_ref, fold(matvec(own, own_ref[...], NN) + matvec(other, other_ref[...], NN)))


def second_row_kernel(core_ref, parts_ref, own_ref, other_ref, own_total_ref, other_total_ref, out_ref, columns):
    own, other = half_columns(core_ref, parts_ref, columns)
    sums = fold(matvec(own, own_ref[...], NN) + matvec(other, other_ref[...], NN))
    spread(out_ref, jnp.concatenate([sums, own_total_ref[...] + other_total_ref[...]], axis=0))


def last_row_kernel(core_ref, parts_ref, own_ref, other_ref, own_product_ref, other_product_ref, out_ref, columns):
    own, other = half_columns(core_ref, parts_ref, columns)
    sums = fold(matvec(own, own_ref[...], NN) + matvec(other, other_ref[...], NN))
    cross = fold(matvec(own, own_product_ref[...], NN) + matvec(other, other_product_ref[...], NN)) * student_scale
    spread(out_ref, jnp.concatenate([sums, cross], axis=0))


def add_kernel(parts_ref, out_ref):
    spread(out_ref, total_of(parts_ref))


def pieces_of(row):
    high = row.astype(bf16).astype(f32)
    middle = (row - high).astype(bf16).astype(f32)
    which = lax.broadcasted_iota(jnp.int32, (16, row.shape[1]), 0)
    pieces = jnp.where(which == 0, high, jnp.where(which == 1, middle, jnp.where(which == 2, row - high - middle, 0.0)))
    return pieces.astype(bf16)


def slope_kernel(which, core_ref, parts_ref, column_ref, total_ref, target_ref, expo_ref, rows_ref, out_ref, columns):
    groups, both, depth = rows_ref.shape
    count = both // 2
    n, width, _ = out_ref.shape
    width = width - 16
    column = half_columns(core_ref, column_ref, columns)[which]
    sums = total_of(parts_ref)
    lines = sums.shape[0] // 2
    row = 1.0 / sums[:lines]
    student_total = total_ref[...]
    partial = jnp.sum(jnp.log(student_total)) - jnp.sum(row * sums[lines:])
    row = unfold(row * student_scale)
    inverse = unfold(student_scale / student_total)
    column = jnp.broadcast_to(column, (8, n * width)).T[:, 0:1]
    for i in range(n):
        grad = jnp.zeros((width, depth), f32)
        for j in range(groups):
            lanes = slice(count * j, count * (j + 1))
            place = (slice(width * i, width * (i + 1)), lanes)
            target = target_ref[place].astype(f32) * column[width * i : width * (i + 1)] * row[:, lanes]
            slope = (expo_ref[place].astype(f32) * inverse[:, lanes] - target).astype(bf16)
            grad = grad + dot(slope, rows_ref[j, count:], NN)
        out_ref[i, :width] = grad.astype(out_ref.dtype)
        out_ref[i, width:] = pieces_of(jnp.full((1, depth), partial, f32)).astype(out_ref.dtype)


def join_kernel(own_ref, other_ref, out_ref):
    n, width, _ = own_ref.shape
    width = width - 16
    for j, i in enumerate(half_turn(n)):
        out_ref[j, :width] = (own_ref[i, :width] + other_ref[i, :width].astype(f32)).astype(bf16)
        pieces = own_ref[i, width:] + other_ref[i, width:].astype(f32)
        out_ref[j, width:] = pieces_of(jnp.sum(pieces, axis=0, keepdims=True))


def finish_kernel(rows, parts_ref, proto_ref, loss_ref, grad_ref):
    width = proto_ref.shape[0]
    unit_grad = parts_ref[0, :width].astype(f32)
    pieces = parts_ref[0, width:].astype(f32)
    for i in range(1, parts_ref.shape[0]):
        unit_grad = unit_grad + parts_ref[i, :width].astype(f32)
        pieces = pieces + parts_ref[i, width:].astype(f32)
    loss_ref[...] = jnp.sum(pieces, axis=0, keepdims=True)[:, :LANES] / rows
    proto = proto_ref[...].astype(f32)
    scale = lax.rsqrt(jnp.sum(proto * proto, axis=1, keepdims=True) + norm_eps)
    unit = proto * scale
    grad_ref[...] = (unit_grad - unit * jnp.sum(unit * unit_grad, axis=1, keepdims=True)) * scale


def half_turn(n):
    return [(i + n // 2) % n for i in range(n)]


def call(kernel, outs, *args, place=None, scratch=(), limit=20):
    vmem = pl.BlockSpec(memory_space=pltpu.VMEM)
    place = place or {}
    return pl.pallas_call(
        kernel,
        out_shape=outs,
        in_specs=[pl.BlockSpec(memory_space=place[i]) if i in place else vmem for i in range(len(args))],
        out_specs=jax.tree.map(lambda _: vmem, outs),
        scratch_shapes=scratch,
        compiler_params=pltpu.CompilerParams(vmem_limit_bytes=limit * 1024 * 1024),
    )(*args)


def per_device(nz, ny, nx, nc, student_patches, teacher_patches, mask_rows, student_proto, teacher_proto):
    shape = jax.ShapeDtypeStruct
    held = pltpu.VMEM
    count = mask_rows.shape[0]
    patches = student_patches.shape
    width, depth = student_proto.shape
    rows = count * nz * ny
    columns = width * nx * nc
    lines, column_lines = rows // LANES, columns // LANES

    orders = {
        "z": half_turn(nz),
        "y": half_turn(ny),
        "x": half_turn(nx),
        ("c", "x"): [c * nx + x for c in reversed(range(nc)) for x in half_turn(nx)],
    }

    def exchange(values, axes):
        return lax.all_to_all(values, axes, 0, 0, axis_index_groups=[orders[axes]], tiled=True)

    def far(values):
        return pltpu.with_memory_space_constraint(values, pltpu.HBM)

    def sems(n):
        return pltpu.SemaphoreType.DMA((n,))

    picked = call(
        rows_kernel,
        shape((nz, 2 * count, depth), bf16),
        far(mask_rows), far(student_patches), far(teacher_patches),
        place={0: pltpu.HBM, 1: pltpu.HBM, 2: pltpu.HBM},
        scratch=[pltpu.SMEM((count,), jnp.int32), pltpu.VMEM(patches, bf16), pltpu.VMEM(patches, bf16), sems(3)],
    )
    late_teacher, late_student, picked = lax.optimization_barrier((teacher_proto, student_proto, picked))
    weights = call(
        weights_kernel,
        shape((2, width, depth), bf16),
        far(late_teacher), far(late_student),
        place={0: pltpu.HBM, 1: pltpu.HBM},
        scratch=[pltpu.VMEM((width, depth), bf16), pltpu.VMEM((width, depth), bf16), sems(2)],
    )
    parts = [weights] + [lax.ppermute(weights, "x", [(i, (i + k) % nx) for i in range(nx)]) for k in range(1, nx)]
    core = lax.axis_index("c").astype(jnp.int32).reshape(1)
    places = (lax.axis_index("x") - jnp.arange(nx, dtype=jnp.int32)) % nx
    places, core, picked = lax.optimization_barrier((places, core, picked))
    picked = exchange(picked, "z")
    picked, parts[2] = lax.optimization_barrier((picked, parts[2]))
    picked = call(divide_kernel, shape((ny, 2 * nz * count, depth), bf16), picked)
    picked = exchange(picked, "y")
    picked, *parts = lax.optimization_barrier((picked, *parts))
    own_weights = call(
        place_kernel,
        shape((nx, *weights.shape), bf16),
        places, *parts,
        place={0: pltpu.SMEM, **{1 + i: pl.ANY for i in range(nx)}},
        scratch=[sems(nx)],
    )
    other_weights = lax.ppermute(own_weights, "c", [(i, (i + 1) % nc) for i in range(nc)])

    matrix = held((nx * width, rows), bf16)
    half_out = (matrix, matrix, matrix, shape((lines, LANES), f32), shape((column_lines // nc, LANES), f32))
    own_target, own_expo, own_product, own_total, own_sums = call(half_kernel, half_out, picked, own_weights)
    other_target, other_expo, other_product, other_total, other_sums = call(half_kernel, half_out, picked, other_weights)
    targets = (own_target, other_target)

    smem = {0: pltpu.SMEM}
    scratch = [pltpu.VMEM((column_lines, LANES), f32)]
    column_out = shape((nx * nc, column_lines, LANES), bf16)
    row_out = shape((ny, lines, LANES), f32)
    rows_out = shape((ny, 2 * lines, LANES), f32)
    column = call(join_first_kernel, column_out, core, own_sums, other_sums, place=smem)
    column = exchange(column, ("c", "x"))
    row = call(row_kernel, row_out, core, column, *targets, place=smem, scratch=scratch)
    row = exchange(row, "y")
    row = call(add_kernel, shape((nz, lines, LANES), f32), row)
    row = exchange(row, "z")

    column = call(column_kernel, column_out, core, row, *targets, place=smem)
    column = exchange(column, ("c", "x"))
    row = call(second_row_kernel, rows_out, core, column, *targets, own_total, other_total, place=smem, scratch=scratch)
    row = exchange(row, "y")
    row = call(add_kernel, shape((nz, 2 * lines, LANES), bf16), row)
    row = exchange(row, "z")

    column, student_total = call(
        third_column_kernel,
        (shape(column_out.shape, f32), shape((lines, LANES), f32)),
        core, row, *targets,
        place=smem,
    )
    column = exchange(column, ("c", "x"))
    row = call(
        last_row_kernel, rows_out, core, column, *targets, own_product, other_product, place=smem, scratch=scratch
    )
    row = exchange(row, "y")
    row = call(add_kernel, shape((nz, 2 * lines, LANES), f32), row)
    row = exchange(row, "z")

    halves = []
    for which, kind, target, expo in ((1, bf16, other_target, other_expo), (0, f32, own_target, own_expo)):
        halves.append(
            call(
                functools.partial(slope_kernel, which),
                shape((nx, width + 16, depth), kind),
                core, row, column, student_total, target, expo, picked,
                place=smem,
                scratch=scratch,
            )
        )
    other = lax.ppermute(halves[0], "c", [(i, (i + 1) % nc) for i in range(nc)])
    grads = call(join_kernel, shape((nx, width + 16, depth), bf16), halves[1], other)
    grads = exchange(grads, "x")
    loss, proto_grad = call(
        lambda *refs: finish_kernel(rows * nx * nc, *refs),
        (shape((1, LANES), f32), shape((width, depth), f32)),
        grads, student_proto,
    )
    return (loss[0, 0], proto_grad)


def solution(mesh):
    nz = mesh.shape["grp"]
    ny, nx, nc = 4, 4, 2
    axes = ("z", "y", "x", "c")
    inner = Mesh(mesh.devices.reshape(nz, ny, nx, nc), axes)
    placed = (P(axes, None), P(axes, None), P(axes), P(axes, None), P(axes, None))
    return jax.shard_map(
        lambda *args: per_device(nz, ny, nx, nc, *args),
        mesh=inner,
        in_specs=placed,
        out_specs=(P(), P(axes, None)),
        check_vma=False,
    )
```

```python
import functools

import jax
import jax.numpy as jnp
from jax import lax
from jax.experimental import pallas as pl
from jax.experimental.pallas import tpu as pltpu
from jax.sharding import Mesh, PartitionSpec as P

LANES = 128

norm_eps = 1e-06
teacher_scale = 1.0 / 0.07
student_scale = 1.0 / 0.1
log2_e = 1.4426950408889634

f32 = jnp.float32
bf16 = jnp.bfloat16
NT = (((1,), (1,)), ((), ()))
NN = (((1,), (0,)), ((), ()))


def dot(a, b, dims):
    return lax.dot_general(a, b, dims, preferred_element_type=f32)


def unit_rows(values):
    values = values.astype(f32)
    return values * lax.rsqrt(jnp.sum(values * values, axis=1, keepdims=True) + norm_eps)


def fold(row):
    n = row.shape[1] // LANES
    return jnp.concatenate([row[:, LANES * i : LANES * (i + 1)] for i in range(n)], axis=0)


def unfold(tile):
    return jnp.concatenate([tile[i : i + 1, :] for i in range(tile.shape[0])], axis=1)


def split_rows(row):
    high = row.astype(bf16).astype(f32)
    which = lax.broadcasted_iota(jnp.int32, (16, row.shape[1]), 0)
    return jnp.where(which == 0, high, jnp.where(which == 1, row - high, 0.0)).astype(bf16)


def matvec(row, matrix, dims):
    return jnp.sum(dot(split_rows(row), matrix, dims), axis=0, keepdims=True)


def lane_sums(row, matrix_ref):
    partial = matrix_ref[:, :LANES].astype(f32) * row[:, :LANES]
    for j in range(1, row.shape[1] // LANES):
        lanes = slice(LANES * j, LANES * (j + 1))
        partial = partial + matrix_ref[:, lanes].astype(f32) * row[:, lanes]
    high = partial.astype(bf16)
    ones = jnp.ones((16, LANES), bf16)
    return (dot(ones, high, NT) + dot(ones, (partial - high.astype(f32)).astype(bf16), NT))[0:1]


def spread(out_ref, tile):
    tile = tile.astype(out_ref.dtype)
    for i in range(out_ref.shape[0]):
        out_ref[i] = tile


def total_of(parts_ref):
    total = parts_ref[0].astype(f32)
    for i in range(1, parts_ref.shape[0]):
        total = total + parts_ref[i].astype(f32)
    return total


def rows_kernel(mask_ref, sp_ref, tp_ref, rows_ref, mask, sp, tp, sems):
    copies = [
        pltpu.make_async_copy(source, target, sems.at[i])
        for i, (source, target) in enumerate(((mask_ref, mask), (tp_ref, tp), (sp_ref, sp)))
    ]
    for copy in copies:
        copy.start()
    count = mask_ref.shape[0]
    patches = sp_ref.shape[0]
    copies[0].wait()
    which = lax.broadcasted_iota(jnp.int32, (count, patches), 0)
    wanted = jnp.zeros((count, patches), jnp.int32)
    for i in range(count):
        wanted = jnp.where(which == i, mask[i], wanted)
    onehot = (lax.broadcasted_iota(jnp.int32, (count, patches), 1) == wanted).astype(f32).astype(bf16)
    copies[1].wait()
    teacher = unit_rows(dot(onehot, tp[...], NN)).astype(bf16)
    copies[2].wait()
    student = unit_rows(dot(onehot, sp[...], NN)).astype(bf16)
    for i in range(rows_ref.shape[0]):
        rows_ref[i, :count] = teacher
        rows_ref[i, count:] = student


def weights_kernel(tw_ref, sw_ref, weights_ref, tw, sw, sems):
    copies = [
        pltpu.make_async_copy(source, target, sems.at[i])
        for i, (source, target) in enumerate(((tw_ref, tw), (sw_ref, sw)))
    ]
    for copy in copies:
        copy.start()
    copies[0].wait()
    weights_ref[0] = unit_rows(tw[...]).astype(bf16)
    copies[1].wait()
    weights_ref[1] = unit_rows(sw[...]).astype(bf16)


def divide_kernel(rows_ref, out_ref):
    n, both, _ = rows_ref.shape
    count = both // 2
    for i in range(n):
        for j in range(out_ref.shape[0]):
            out_ref[j, count * i : count * (i + 1)] = rows_ref[i, :count]
            out_ref[j, count * (n + i) : count * (n + i + 1)] = rows_ref[i, count:]


def place_kernel(place_ref, *refs):
    *parts, out_ref, sems = refs
    copies = [
        pltpu.make_async_copy(part, out_ref.at[place_ref[i]], sems.at[i]) for i, part in enumerate(parts)
    ]
    for copy in copies:
        copy.start()
    for copy in copies:
        copy.wait()


def half_kernel(rows_ref, weights_ref, target_ref, expo_ref, product_ref, total_ref, sums_ref):
    groups, both, _ = rows_ref.shape
    count = both // 2
    nx, _, width, _ = weights_ref.shape
    for j in range(groups):
        total = jnp.zeros((1, count), f32)
        for i in range(nx):
            place = (slice(width * i, width * (i + 1)), slice(count * j, count * (j + 1)))
            target = jnp.exp2(dot(weights_ref[i, 0], rows_ref[j, :count], NT) * (teacher_scale * log2_e))
            score = dot(weights_ref[i, 1], rows_ref[j, count:], NT)
            expo = jnp.exp2(score * (student_scale * log2_e))
            total = total + jnp.sum(expo, axis=0, keepdims=True)
            target_ref[place] = target.astype(bf16)
            expo_ref[place] = expo.astype(bf16)
            product_ref[place] = (target * score).astype(bf16)
        per = count // LANES
        total_ref[per * j : per * (j + 1)] = fold(total)
    sums_ref[...] = fold(matvec(jnp.ones((1, groups * count), f32), target_ref[...], NT))


def spread_halves(core_ref, out_ref, own, other):
    first = core_ref[0] == 0
    spread(out_ref, jnp.concatenate([jnp.where(first, own, other), jnp.where(first, other, own)], axis=0))


def half_columns(core_ref, parts_ref, columns):
    columns[...] = 1.0 / total_of(parts_ref)
    core = core_ref[0]
    lines = columns.shape[0] // 2
    own = columns[pl.ds(pl.multiple_of(core * lines, lines), lines), :]
    other = columns[pl.ds(pl.multiple_of((1 - core) * lines, lines), lines), :]
    return unfold(own), unfold(other)


def join_first_kernel(core_ref, own_ref, other_ref, column_ref):
    spread_halves(core_ref, column_ref, own_ref[...], other_ref[...])


def column_kernel(core_ref, parts_ref, own_ref, other_ref, column_ref):
    row = unfold(1.0 / total_of(parts_ref))
    spread_halves(core_ref, column_ref, fold(lane_sums(row, own_ref)), fold(lane_sums(row, other_ref)))


def third_column_kernel(core_ref, parts_ref, own_ref, other_ref, column_ref, total_ref):
    both = total_of(parts_ref)
    lines = both.shape[0] // 2
    row = unfold(1.0 / both[:lines])
    spread_halves(core_ref, column_ref, fold(lane_sums(row, own_ref)), fold(lane_sums(row, other_ref)))
    total_ref[...] = both[lines:]


def row_kernel(core_ref, parts_ref, own_ref, other_ref, out_ref, columns):
    own, other = half_columns(core_ref, parts_ref, columns)
    spread(out_ref, fold(matvec(own, own_ref[...], NN) + matvec(other, other_ref[...], NN)))


def second_row_kernel(core_ref, parts_ref, own_ref, other_ref, own_total_ref, other_total_ref, out_ref, columns):
    own, other = half_columns(core_ref, parts_ref, columns)
    sums = fold(matvec(own, own_ref[...], NN) + matvec(other, other_ref[...], NN))
    spread(out_ref, jnp.concatenate([sums, own_total_ref[...] + other_total_ref[...]], axis=0))


def last_row_kernel(core_ref, parts_ref, own_ref, other_ref, own_product_ref, other_product_ref, out_ref, columns):
    own, other = half_columns(core_ref, parts_ref, columns)
    sums = fold(matvec(own, own_ref[...], NN) + matvec(other, other_ref[...], NN))
    cross = fold(matvec(own, own_product_ref[...], NN) + matvec(other, other_product_ref[...], NN)) * student_scale
    spread(out_ref, jnp.concatenate([sums, cross], axis=0))


def add_kernel(parts_ref, out_ref):
    spread(out_ref, total_of(parts_ref))


def pieces_of(row):
    high = row.astype(bf16).astype(f32)
    middle = (row - high).astype(bf16).astype(f32)
    which = lax.broadcasted_iota(jnp.int32, (16, row.shape[1]), 0)
    pieces = jnp.where(which == 0, high, jnp.where(which == 1, middle, jnp.where(which == 2, row - high - middle, 0.0)))
    return pieces.astype(bf16)


def slope_kernel(which, core_ref, parts_ref, column_ref, total_ref, target_ref, expo_ref, rows_ref, out_ref, columns):
    groups, both, depth = rows_ref.shape
    count = both // 2
    n, width, _ = out_ref.shape
    width = width - 16
    column = half_columns(core_ref, column_ref, columns)[which]
    sums = total_of(parts_ref)
    lines = sums.shape[0] // 2
    row = 1.0 / sums[:lines]
    student_total = total_ref[...]
    partial = jnp.sum(jnp.log(student_total)) - jnp.sum(row * sums[lines:])
    row = unfold(row * student_scale)
    inverse = unfold(student_scale / student_total)
    column = jnp.broadcast_to(column, (8, n * width)).T[:, 0:1]
    for i in range(n):
        grad = jnp.zeros((width, depth), f32)
        for j in range(groups):
            lanes = slice(count * j, count * (j + 1))
            place = (slice(width * i, width * (i + 1)), lanes)
            target = target_ref[place].astype(f32) * column[width * i : width * (i + 1)] * row[:, lanes]
            slope = (expo_ref[place].astype(f32) * inverse[:, lanes] - target).astype(bf16)
            grad = grad + dot(slope, rows_ref[j, count:], NN)
        out_ref[i, :width] = grad.astype(out_ref.dtype)
        out_ref[i, width:] = pieces_of(jnp.full((1, depth), partial, f32)).astype(out_ref.dtype)


def join_kernel(own_ref, other_ref, out_ref):
    n, width, _ = own_ref.shape
    width = width - 16
    for j, i in enumerate(half_turn(n)):
        out_ref[j, :width] = (own_ref[i, :width] + other_ref[i, :width].astype(f32)).astype(bf16)
        pieces = own_ref[i, width:] + other_ref[i, width:].astype(f32)
        out_ref[j, width:] = pieces_of(jnp.sum(pieces, axis=0, keepdims=True))


def finish_kernel(rows, parts_ref, proto_ref, loss_ref, grad_ref):
    width = proto_ref.shape[0]
    unit_grad = parts_ref[0, :width].astype(f32)
    pieces = parts_ref[0, width:].astype(f32)
    for i in range(1, parts_ref.shape[0]):
        unit_grad = unit_grad + parts_ref[i, :width].astype(f32)
        pieces = pieces + parts_ref[i, width:].astype(f32)
    loss_ref[...] = jnp.sum(pieces, axis=0, keepdims=True)[:, :LANES] / rows
    proto = proto_ref[...].astype(f32)
    scale = lax.rsqrt(jnp.sum(proto * proto, axis=1, keepdims=True) + norm_eps)
    unit = proto * scale
    grad_ref[...] = (unit_grad - unit * jnp.sum(unit * unit_grad, axis=1, keepdims=True)) * scale


def half_turn(n):
    return [(i + n // 2) % n for i in range(n)]


def call(kernel, outs, *args, place=None, scratch=(), limit=20):
    vmem = pl.BlockSpec(memory_space=pltpu.VMEM)
    place = place or {}
    return pl.pallas_call(
        kernel,
        out_shape=outs,
        in_specs=[pl.BlockSpec(memory_space=place[i]) if i in place else vmem for i in range(len(args))],
        out_specs=jax.tree.map(lambda _: vmem, outs),
        scratch_shapes=scratch,
        compiler_params=pltpu.CompilerParams(vmem_limit_bytes=limit * 1024 * 1024),
    )(*args)


def per_device(nz, ny, nx, nc, student_patches, teacher_patches, mask_rows, student_proto, teacher_proto):
    shape = jax.ShapeDtypeStruct
    held = pltpu.VMEM
    count = mask_rows.shape[0]
    patches = student_patches.shape
    width, depth = student_proto.shape
    rows = count * nz * ny
    columns = width * nx * nc
    lines, column_lines = rows // LANES, columns // LANES

    orders = {
        "z": [(i + 10) % nz for i in range(nz)],
        "y": half_turn(ny),
        "x": half_turn(nx),
        ("c", "x"): [c * nx + x for c in reversed(range(nc)) for x in half_turn(nx)],
    }

    def exchange(values, axes):
        return lax.all_to_all(values, axes, 0, 0, axis_index_groups=[orders[axes]], tiled=True)

    def far(values):
        return pltpu.with_memory_space_constraint(values, pltpu.HBM)

    def sems(n):
        return pltpu.SemaphoreType.DMA((n,))

    picked = call(
        rows_kernel,
        shape((nz, 2 * count, depth), bf16),
        far(mask_rows), far(student_patches), far(teacher_patches),
        place={0: pltpu.HBM, 1: pltpu.HBM, 2: pltpu.HBM},
        scratch=[pltpu.SMEM((count,), jnp.int32), pltpu.VMEM(patches, bf16), pltpu.VMEM(patches, bf16), sems(3)],
    )
    late_teacher, late_student, picked = lax.optimization_barrier((teacher_proto, student_proto, picked))
    weights = call(
        weights_kernel,
        shape((2, width, depth), bf16),
        far(late_teacher), far(late_student),
        place={0: pltpu.HBM, 1: pltpu.HBM},
        scratch=[pltpu.VMEM((width, depth), bf16), pltpu.VMEM((width, depth), bf16), sems(2)],
    )
    parts = [weights] + [lax.ppermute(weights, "x", [(i, (i + k) % nx) for i in range(nx)]) for k in range(1, nx)]
    core = lax.axis_index("c").astype(jnp.int32).reshape(1)
    places = (lax.axis_index("x") - jnp.arange(nx, dtype=jnp.int32)) % nx
    places, core, picked = lax.optimization_barrier((places, core, picked))
    picked = exchange(picked, "z")
    picked, parts[2] = lax.optimization_barrier((picked, parts[2]))
    picked = call(divide_kernel, shape((ny, 2 * nz * count, depth), bf16), picked)
    picked = exchange(picked, "y")
    picked, *parts = lax.optimization_barrier((picked, *parts))
    own_weights = call(
        place_kernel,
        shape((nx, *weights.shape), bf16),
        places, *parts,
        place={0: pltpu.SMEM, **{1 + i: pl.ANY for i in range(nx)}},
        scratch=[sems(nx)],
    )
    other_weights = lax.ppermute(own_weights, "c", [(i, (i + 1) % nc) for i in range(nc)])

    matrix = held((nx * width, rows), bf16)
    half_out = (matrix, matrix, matrix, shape((lines, LANES), f32), shape((column_lines // nc, LANES), f32))
    own_target, own_expo, own_product, own_total, own_sums = call(half_kernel, half_out, picked, own_weights)
    other_target, other_expo, other_product, other_total, other_sums = call(half_kernel, half_out, picked, other_weights)
    targets = (own_target, other_target)

    smem = {0: pltpu.SMEM}
    scratch = [pltpu.VMEM((column_lines, LANES), f32)]
    column_out = shape((nx * nc, column_lines, LANES), bf16)
    row_out = shape((ny, lines, LANES), f32)
    rows_out = shape((ny, 2 * lines, LANES), f32)
    column = call(join_first_kernel, column_out, core, own_sums, other_sums, place=smem)
    column = exchange(column, ("c", "x"))
    row = call(row_kernel, row_out, core, column, *targets, place=smem, scratch=scratch)
    row = exchange(row, "y")
    row = call(add_kernel, shape((nz, lines, LANES), f32), row)
    row = exchange(row, "z")

    column = call(column_kernel, column_out, core, row, *targets, place=smem)
    column = exchange(column, ("c", "x"))
    row = call(second_row_kernel, shape(rows_out.shape, bf16), core, column, *targets, own_total, other_total, place=smem, scratch=scratch)
    row = exchange(row, "y")
    row = call(add_kernel, shape((nz, 2 * lines, LANES), bf16), row)
    row = exchange(row, "z")

    column, student_total = call(
        third_column_kernel, (column_out, shape((lines, LANES), f32)), core, row, *targets, place=smem
    )
    column = exchange(column, ("c", "x"))
    row = call(
        last_row_kernel, rows_out, core, column, *targets, own_product, other_product, place=smem, scratch=scratch
    )
    row = exchange(row, "y")
    row = call(add_kernel, shape((nz, 2 * lines, LANES), bf16), row)
    row = exchange(row, "z")

    halves = []
    for which, kind, target, expo in ((1, bf16, other_target, other_expo), (0, f32, own_target, own_expo)):
        halves.append(
            call(
                functools.partial(slope_kernel, which),
                shape((nx, width + 16, depth), kind),
                core, row, column, student_total, target, expo, picked,
                place=smem,
                scratch=scratch,
            )
        )
    other = lax.ppermute(halves[0], "c", [(i, (i + 1) % nc) for i in range(nc)])
    grads = call(join_kernel, shape((nx, width + 16, depth), bf16), halves[1], other)
    grads = exchange(grads, "x")
    loss, proto_grad = call(
        lambda *refs: finish_kernel(rows * nx * nc, *refs),
        (shape((1, LANES), f32), shape((width, depth), f32)),
        grads, student_proto,
    )
    return (loss[0, 0], proto_grad)


def solution(mesh):
    nz = mesh.shape["grp"]
    ny, nx, nc = 4, 4, 2
    axes = ("z", "y", "x", "c")
    inner = Mesh(mesh.devices.reshape(nz, ny, nx, nc), axes)
    placed = (P(axes, None), P(axes, None), P(axes), P(axes, None), P(axes, None))
    return jax.shard_map(
        lambda *args: per_device(nz, ny, nx, nc, *args),
        mesh=inner,
        in_specs=placed,
        out_specs=(P(), P(axes, None)),
        check_vma=False,
    )
```

```python
import functools

import jax
import jax.numpy as jnp
from jax import lax
from jax.experimental import pallas as pl
from jax.experimental.pallas import tpu as pltpu
from jax.sharding import Mesh, PartitionSpec as P

LANES = 128

norm_eps = 1e-06
teacher_scale = 1.0 / 0.07
student_scale = 1.0 / 0.1
log2_e = 1.4426950408889634

f32 = jnp.float32
bf16 = jnp.bfloat16
NT = (((1,), (1,)), ((), ()))
NN = (((1,), (0,)), ((), ()))


def dot(a, b, dims):
    return lax.dot_general(a, b, dims, preferred_element_type=f32)


def unit_rows(values):
    values = values.astype(f32)
    return values * lax.rsqrt(jnp.sum(values * values, axis=1, keepdims=True) + norm_eps)


def fold(row):
    n = row.shape[1] // LANES
    return jnp.concatenate([row[:, LANES * i : LANES * (i + 1)] for i in range(n)], axis=0)


def unfold(tile):
    return jnp.concatenate([tile[i : i + 1, :] for i in range(tile.shape[0])], axis=1)


def split_rows(row):
    high = row.astype(bf16).astype(f32)
    which = lax.broadcasted_iota(jnp.int32, (16, row.shape[1]), 0)
    return jnp.where(which == 0, high, jnp.where(which == 1, row - high, 0.0)).astype(bf16)


def matvec(row, matrix, dims):
    return jnp.sum(dot(split_rows(row), matrix, dims), axis=0, keepdims=True)


def lane_sums(row, matrix_ref):
    partial = matrix_ref[:, :LANES].astype(f32) * row[:, :LANES]
    for j in range(1, row.shape[1] // LANES):
        lanes = slice(LANES * j, LANES * (j + 1))
        partial = partial + matrix_ref[:, lanes].astype(f32) * row[:, lanes]
    high = partial.astype(bf16)
    ones = jnp.ones((16, LANES), bf16)
    return (dot(ones, high, NT) + dot(ones, (partial - high.astype(f32)).astype(bf16), NT))[0:1]


def spread(out_ref, tile):
    tile = tile.astype(out_ref.dtype)
    for i in range(out_ref.shape[0]):
        out_ref[i] = tile


def total_of(parts_ref):
    total = parts_ref[0].astype(f32)
    for i in range(1, parts_ref.shape[0]):
        total = total + parts_ref[i].astype(f32)
    return total


def rows_kernel(mask_ref, sp_ref, tp_ref, rows_ref, mask, sp, tp, sems):
    copies = [
        pltpu.make_async_copy(source, target, sems.at[i])
        for i, (source, target) in enumerate(((mask_ref, mask), (tp_ref, tp), (sp_ref, sp)))
    ]
    for copy in copies:
        copy.start()
    count = mask_ref.shape[0]
    patches = sp_ref.shape[0]
    copies[0].wait()
    which = lax.broadcasted_iota(jnp.int32, (count, patches), 0)
    wanted = jnp.zeros((count, patches), jnp.int32)
    for i in range(count):
        wanted = jnp.where(which == i, mask[i], wanted)
    onehot = (lax.broadcasted_iota(jnp.int32, (count, patches), 1) == wanted).astype(f32).astype(bf16)
    copies[1].wait()
    teacher = unit_rows(dot(onehot, tp[...], NN)).astype(bf16)
    copies[2].wait()
    student = unit_rows(dot(onehot, sp[...], NN)).astype(bf16)
    for i in range(rows_ref.shape[0]):
        rows_ref[i, :count] = teacher
        rows_ref[i, count:] = student


def weights_kernel(tw_ref, sw_ref, weights_ref, tw, sw, sems):
    copies = [
        pltpu.make_async_copy(source, target, sems.at[i])
        for i, (source, target) in enumerate(((tw_ref, tw), (sw_ref, sw)))
    ]
    for copy in copies:
        copy.start()
    copies[0].wait()
    weights_ref[0] = unit_rows(tw[...]).astype(bf16)
    copies[1].wait()
    weights_ref[1] = unit_rows(sw[...]).astype(bf16)


def divide_kernel(rows_ref, out_ref):
    n, both, _ = rows_ref.shape
    count = both // 2
    for i in range(n):
        for j in range(out_ref.shape[0]):
            out_ref[j, count * i : count * (i + 1)] = rows_ref[i, :count]
            out_ref[j, count * (n + i) : count * (n + i + 1)] = rows_ref[i, count:]


def place_kernel(place_ref, *refs):
    *parts, out_ref, sems = refs
    copies = [
        pltpu.make_async_copy(part, out_ref.at[place_ref[i]], sems.at[i]) for i, part in enumerate(parts)
    ]
    for copy in copies:
        copy.start()
    for copy in copies:
        copy.wait()


def half_kernel(rows_ref, weights_ref, target_ref, expo_ref, product_ref, total_ref, sums_ref):
    groups, both, _ = rows_ref.shape
    count = both // 2
    nx, _, width, _ = weights_ref.shape
    for j in range(groups):
        total = jnp.zeros((1, count), f32)
        for i in range(nx):
            place = (slice(width * i, width * (i + 1)), slice(count * j, count * (j + 1)))
            target = jnp.exp2(dot(weights_ref[i, 0], rows_ref[j, :count], NT) * (teacher_scale * log2_e))
            score = dot(weights_ref[i, 1], rows_ref[j, count:], NT)
            expo = jnp.exp2(score * (student_scale * log2_e))
            total = total + jnp.sum(expo, axis=0, keepdims=True)
            target_ref[place] = target.astype(bf16)
            expo_ref[place] = expo.astype(bf16)
            product_ref[place] = (target * score).astype(bf16)
        per = count // LANES
        total_ref[per * j : per * (j + 1)] = fold(total)
    sums_ref[...] = fold(matvec(jnp.ones((1, groups * count), f32), target_ref[...], NT))


def spread_halves(core_ref, out_ref, own, other):
    first = core_ref[0] == 0
    spread(out_ref, jnp.concatenate([jnp.where(first, own, other), jnp.where(first, other, own)], axis=0))


def half_columns(core_ref, parts_ref, columns):
    columns[...] = 1.0 / total_of(parts_ref)
    core = core_ref[0]
    lines = columns.shape[0] // 2
    own = columns[pl.ds(pl.multiple_of(core * lines, lines), lines), :]
    other = columns[pl.ds(pl.multiple_of((1 - core) * lines, lines), lines), :]
    return unfold(own), unfold(other)


def join_first_kernel(core_ref, own_ref, other_ref, column_ref):
    spread_halves(core_ref, column_ref, own_ref[...], other_ref[...])


def column_kernel(core_ref, parts_ref, own_ref, other_ref, column_ref):
    row = unfold(1.0 / total_of(parts_ref))
    spread_halves(core_ref, column_ref, fold(lane_sums(row, own_ref)), fold(lane_sums(row, other_ref)))


def third_column_kernel(core_ref, parts_ref, own_ref, other_ref, column_ref, total_ref):
    both = total_of(parts_ref)
    lines = both.shape[0] // 2
    row = unfold(1.0 / both[:lines])
    spread_halves(core_ref, column_ref, fold(lane_sums(row, own_ref)), fold(lane_sums(row, other_ref)))
    total_ref[...] = both[lines:]


def row_kernel(core_ref, parts_ref, own_ref, other_ref, out_ref, columns):
    own, other = half_columns(core_ref, parts_ref, columns)
    spread(out_ref, fold(matvec(own, own_ref[...], NN) + matvec(other, other_ref[...], NN)))


def second_row_kernel(core_ref, parts_ref, own_ref, other_ref, own_total_ref, other_total_ref, out_ref, columns):
    own, other = half_columns(core_ref, parts_ref, columns)
    sums = fold(matvec(own, own_ref[...], NN) + matvec(other, other_ref[...], NN))
    spread(out_ref, jnp.concatenate([sums, own_total_ref[...] + other_total_ref[...]], axis=0))


def last_row_kernel(core_ref, parts_ref, own_ref, other_ref, own_product_ref, other_product_ref, out_ref, columns):
    own, other = half_columns(core_ref, parts_ref, columns)
    sums = fold(matvec(own, own_ref[...], NN) + matvec(other, other_ref[...], NN))
    cross = fold(matvec(own, own_product_ref[...], NN) + matvec(other, other_product_ref[...], NN)) * student_scale
    spread(out_ref, jnp.concatenate([sums, cross], axis=0))


def add_kernel(parts_ref, out_ref):
    spread(out_ref, total_of(parts_ref))


def pieces_of(row):
    high = row.astype(bf16).astype(f32)
    middle = (row - high).astype(bf16).astype(f32)
    which = lax.broadcasted_iota(jnp.int32, (16, row.shape[1]), 0)
    pieces = jnp.where(which == 0, high, jnp.where(which == 1, middle, jnp.where(which == 2, row - high - middle, 0.0)))
    return pieces.astype(bf16)


def slope_kernel(which, core_ref, parts_ref, column_ref, total_ref, target_ref, expo_ref, rows_ref, out_ref, columns):
    groups, both, depth = rows_ref.shape
    count = both // 2
    n, width, _ = out_ref.shape
    width = width - 16
    column = half_columns(core_ref, column_ref, columns)[which]
    sums = total_of(parts_ref)
    lines = sums.shape[0] // 2
    row = 1.0 / sums[:lines]
    student_total = total_ref[...]
    partial = jnp.sum(jnp.log(student_total)) - jnp.sum(row * sums[lines:])
    row = unfold(row * student_scale)
    inverse = unfold(student_scale / student_total)
    column = jnp.broadcast_to(column, (8, n * width)).T[:, 0:1]
    for i in range(n):
        grad = jnp.zeros((width, depth), f32)
        for j in range(groups):
            lanes = slice(count * j, count * (j + 1))
            place = (slice(width * i, width * (i + 1)), lanes)
            target = target_ref[place].astype(f32) * column[width * i : width * (i + 1)] * row[:, lanes]
            slope = (expo_ref[place].astype(f32) * inverse[:, lanes] - target).astype(bf16)
            grad = grad + dot(slope, rows_ref[j, count:], NN)
        out_ref[i, :width] = grad.astype(out_ref.dtype)
        out_ref[i, width:] = pieces_of(jnp.full((1, depth), partial, f32)).astype(out_ref.dtype)


def join_kernel(own_ref, other_ref, out_ref):
    n, width, _ = own_ref.shape
    width = width - 16
    for j, i in enumerate(half_turn(n)):
        out_ref[j, :width] = (own_ref[i, :width] + other_ref[i, :width].astype(f32)).astype(bf16)
        pieces = own_ref[i, width:] + other_ref[i, width:].astype(f32)
        out_ref[j, width:] = pieces_of(jnp.sum(pieces, axis=0, keepdims=True))


def finish_kernel(rows, parts_ref, proto_ref, loss_ref, grad_ref):
    width = proto_ref.shape[0]
    unit_grad = parts_ref[0, :width].astype(f32)
    pieces = parts_ref[0, width:].astype(f32)
    for i in range(1, parts_ref.shape[0]):
        unit_grad = unit_grad + parts_ref[i, :width].astype(f32)
        pieces = pieces + parts_ref[i, width:].astype(f32)
    loss_ref[...] = jnp.sum(pieces, axis=0, keepdims=True)[:, :LANES] / rows
    proto = proto_ref[...].astype(f32)
    scale = lax.rsqrt(jnp.sum(proto * proto, axis=1, keepdims=True) + norm_eps)
    unit = proto * scale
    grad_ref[...] = (unit_grad - unit * jnp.sum(unit * unit_grad, axis=1, keepdims=True)) * scale


def half_turn(n):
    return [(i + n // 2) % n for i in range(n)]


def call(kernel, outs, *args, place=None, scratch=(), limit=20):
    vmem = pl.BlockSpec(memory_space=pltpu.VMEM)
    place = place or {}
    return pl.pallas_call(
        kernel,
        out_shape=outs,
        in_specs=[pl.BlockSpec(memory_space=place[i]) if i in place else vmem for i in range(len(args))],
        out_specs=jax.tree.map(lambda _: vmem, outs),
        scratch_shapes=scratch,
        compiler_params=pltpu.CompilerParams(vmem_limit_bytes=limit * 1024 * 1024),
    )(*args)


def per_device(nz, ny, nx, nc, student_patches, teacher_patches, mask_rows, student_proto, teacher_proto):
    shape = jax.ShapeDtypeStruct
    held = pltpu.VMEM
    count = mask_rows.shape[0]
    patches = student_patches.shape
    width, depth = student_proto.shape
    rows = count * nz * ny
    columns = width * nx * nc
    lines, column_lines = rows // LANES, columns // LANES

    orders = {
        "z": [(i + 10) % nz for i in range(nz)],
        "y": half_turn(ny),
        "x": half_turn(nx),
        ("c", "x"): [c * nx + x for c in range(nc) for x in half_turn(nx)],
    }

    def exchange(values, axes):
        return lax.all_to_all(values, axes, 0, 0, axis_index_groups=[orders[axes]], tiled=True)

    def far(values):
        return pltpu.with_memory_space_constraint(values, pltpu.HBM)

    def sems(n):
        return pltpu.SemaphoreType.DMA((n,))

    picked = call(
        rows_kernel,
        shape((nz, 2 * count, depth), bf16),
        far(mask_rows), far(student_patches), far(teacher_patches),
        place={0: pltpu.HBM, 1: pltpu.HBM, 2: pltpu.HBM},
        scratch=[pltpu.SMEM((count,), jnp.int32), pltpu.VMEM(patches, bf16), pltpu.VMEM(patches, bf16), sems(3)],
    )
    late_teacher, late_student, picked = lax.optimization_barrier((teacher_proto, student_proto, picked))
    weights = call(
        weights_kernel,
        shape((2, width, depth), bf16),
        far(late_teacher), far(late_student),
        place={0: pltpu.HBM, 1: pltpu.HBM},
        scratch=[pltpu.VMEM((width, depth), bf16), pltpu.VMEM((width, depth), bf16), sems(2)],
    )
    parts = [weights] + [lax.ppermute(weights, "x", [(i, (i + k) % nx) for i in range(nx)]) for k in range(1, nx)]
    core = lax.axis_index("c").astype(jnp.int32).reshape(1)
    places = (lax.axis_index("x") - jnp.arange(nx, dtype=jnp.int32)) % nx
    places, core, picked = lax.optimization_barrier((places, core, picked))
    picked = exchange(picked, "z")
    picked, parts[2] = lax.optimization_barrier((picked, parts[2]))
    picked = call(divide_kernel, shape((ny, 2 * nz * count, depth), bf16), picked)
    picked = exchange(picked, "y")
    picked, *parts = lax.optimization_barrier((picked, *parts))
    own_weights = call(
        place_kernel,
        shape((nx, *weights.shape), bf16),
        places, *parts,
        place={0: pltpu.SMEM, **{1 + i: pl.ANY for i in range(nx)}},
        scratch=[sems(nx)],
    )
    other_weights = lax.ppermute(own_weights, "c", [(i, (i + 1) % nc) for i in range(nc)])

    matrix = held((nx * width, rows), bf16)
    half_out = (matrix, matrix, matrix, shape((lines, LANES), f32), shape((column_lines // nc, LANES), f32))
    own_target, own_expo, own_product, own_total, own_sums = call(half_kernel, half_out, picked, own_weights)
    other_target, other_expo, other_product, other_total, other_sums = call(half_kernel, half_out, picked, other_weights)
    targets = (own_target, other_target)

    smem = {0: pltpu.SMEM}
    scratch = [pltpu.VMEM((column_lines, LANES), f32)]
    column_out = shape((nx * nc, column_lines, LANES), bf16)
    row_out = shape((ny, lines, LANES), f32)
    rows_out = shape((ny, 2 * lines, LANES), f32)
    column = call(join_first_kernel, column_out, core, own_sums, other_sums, place=smem)
    column = exchange(column, ("c", "x"))
    row = call(row_kernel, row_out, core, column, *targets, place=smem, scratch=scratch)
    row = exchange(row, "y")
    row = call(add_kernel, shape((nz, lines, LANES), f32), row)
    row = exchange(row, "z")

    column = call(column_kernel, column_out, core, row, *targets, place=smem)
    column = exchange(column, ("c", "x"))
    row = call(second_row_kernel, shape(rows_out.shape, bf16), core, column, *targets, own_total, other_total, place=smem, scratch=scratch)
    row = exchange(row, "y")
    row = call(add_kernel, shape((nz, 2 * lines, LANES), bf16), row)
    row = exchange(row, "z")

    column, student_total = call(
        third_column_kernel, (column_out, shape((lines, LANES), f32)), core, row, *targets, place=smem
    )
    column = exchange(column, ("c", "x"))
    row = call(
        last_row_kernel, rows_out, core, column, *targets, own_product, other_product, place=smem, scratch=scratch
    )
    row = exchange(row, "y")
    row = call(add_kernel, shape((nz, 2 * lines, LANES), bf16), row)
    row = exchange(row, "z")

    halves = []
    for which, kind, target, expo in ((1, bf16, other_target, other_expo), (0, f32, own_target, own_expo)):
        halves.append(
            call(
                functools.partial(slope_kernel, which),
                shape((nx, width + 16, depth), kind),
                core, row, column, student_total, target, expo, picked,
                place=smem,
                scratch=scratch,
            )
        )
    other = lax.ppermute(halves[0], "c", [(i, (i + 1) % nc) for i in range(nc)])
    grads = call(join_kernel, shape((nx, width + 16, depth), bf16), halves[1], other)
    grads = exchange(grads, "x")
    loss, proto_grad = call(
        lambda *refs: finish_kernel(rows * nx * nc, *refs),
        (shape((1, LANES), f32), shape((width, depth), f32)),
        grads, student_proto,
    )
    return (loss[0, 0], proto_grad)


def solution(mesh):
    nz = mesh.shape["grp"]
    ny, nx, nc = 4, 4, 2
    axes = ("z", "y", "x", "c")
    inner = Mesh(mesh.devices.reshape(nz, ny, nx, nc), axes)
    placed = (P(axes, None), P(axes, None), P(axes), P(axes, None), P(axes, None))
    return jax.shard_map(
        lambda *args: per_device(nz, ny, nx, nc, *args),
        mesh=inner,
        in_specs=placed,
        out_specs=(P(), P(axes, None)),
        check_vma=False,
    )
```
